32 devices in a mesh: band: 2 (over x), stn: 8 (over z, y), tile: 2 (over core).
Axes of the slice: x: 2, y: 2, z: 4, core: 2. Of those that a mesh axis runs over, the one named last changes fastest.
Arguments:
- raw_samples: float32 [2, 4096, 8240], P(None, ('band', 'stn', 'tile')), parts along dimension 1, may hold values from -6 to 6
- prototype: float32 [64], replicated, may hold values from -0.75 to 0.75
- beam_weight: bfloat16 [2, 512, 4096], P(None, None, ('band', 'stn', 'tile')), parts along dimension 2, may hold values from -0.09375 to 0.09375
Outputs:
- visibility: bfloat16 [64, 2, 2048, 2048], P(('band', 'stn'), None, None, 'tile'), parts along dimension 0
- beam_out: float32 [2, 64, 512, 256], P(None, ('band', 'stn'), 'tile'), parts along dimension 1
The draws below stay inside these ranges and needn't reach their ends.
There are 2 independent parts, one for each index of `band`. The reference program is written for one: setup_inputs(seed, part) draws one part's arguments, and reference() takes and returns one part's arrays. A program takes and returns all parts, laid end to end along the dimension named above; an argument that names none is the same for every part. Nothing has to cross between parts.
All inputs are finite; a program needn't handle non-finite values.
Results may differ from the reference program's by a relative error of at most 0.0055.
Values may be sent and summed in bfloat16 or wider, within the bound.
No kernel may reach another device: no remote copies, remote signals or barrier semaphores. Data moves between devices by JAX's collectives and lax.ppermute only.
A program may use at most 192 MiB of HBM per device.

```python
import math
import jax
import jax.numpy as jnp
from jax import lax

INPUTS = 2048
FINE = 16
TAPS = 4
NBEAM = 512
DUMPS = 2
MD = 256
STN_BLOCKS = 8
CORE_BLOCKS = 2
SAMPLES = 8240


def block_levels(stream_key, shape, pieces, smallest, top_value):
    factor_of, own = 1.0, jax.random.fold_in(stream_key, 6)
    for dim, parts in pieces:
        steps = jnp.exp(jax.random.uniform(jax.random.fold_in(own, dim), (parts,), jnp.float32, smallest / len(pieces), top_value / len(pieces)))
        factor_of = factor_of * jnp.repeat(steps, shape[dim] // parts).reshape([-1 if axis == dim else 1 for axis in range(len(shape))])
    return factor_of


def bell_draw(stream_key, shape, spread, limit, pieces=(), held_as=jnp.bfloat16):
    result = jax.random.normal(stream_key, shape, jnp.float32) * spread
    if len(pieces) > 0:
        result = block_levels(stream_key, shape, pieces, -0.22, 0.18) * result
    return jnp.clip(result, min=-limit, max=limit).astype(held_as)


def setup_inputs(seed: int = 0, part: int = 0) -> dict:
    key_of = jax.random.split(jax.random.key(seed), 4)
    part_keys = jax.random.split(jax.random.fold_in(key_of[3], part), 4)
    raw_samples = bell_draw(part_keys[0], (2, INPUTS, SAMPLES), 1.0, 6.0, ((1, 16),), jnp.float32)
    prototype = bell_draw(key_of[1], (TAPS * FINE,), (TAPS * FINE) ** -0.5, 0.75, (), jnp.float32)
    beam_weight = bell_draw(part_keys[2], (2, NBEAM, INPUTS), (2 * INPUTS) ** -0.5, 0.09375, ((2, 16),))
    return {"raw_samples": raw_samples, "prototype": prototype, "beam_weight": beam_weight}


def filter_table(prototype):
    taps_fine = prototype.shape[0]
    sample = jnp.arange(taps_fine, dtype=jnp.int32) % FINE
    channel = jnp.arange(FINE, dtype=jnp.int32)
    phase_index = (sample[:, None] * channel[None, :]) % FINE
    phase_angle = phase_index.astype(jnp.float32) * (2.0 * math.pi / FINE)
    return prototype[:, None] * jnp.cos(phase_angle), -prototype[:, None] * jnp.sin(phase_angle)


def channelize(raw_samples, prototype):
    table_re, table_im = filter_table(prototype)
    inputs_here = raw_samples.shape[1]
    frames = DUMPS * MD
    shaped = raw_samples.reshape(2, inputs_here, frames + TAPS - 1, FINE)
    windows = jnp.concatenate([shaped[:, :, offset:offset + frames, :] for offset in range(TAPS)], axis=3)
    highest = lax.Precision.HIGHEST
    spec_re = jnp.einsum('bmn,nk->kbm', windows[0], table_re, precision=highest) - jnp.einsum('bmn,nk->kbm', windows[1], table_im, precision=highest)
    spec_im = jnp.einsum('bmn,nk->kbm', windows[0], table_im, precision=highest) + jnp.einsum('bmn,nk->kbm', windows[1], table_re, precision=highest)
    return spec_re, spec_im


def reference(raw_samples, prototype, beam_weight):
    spec_re, spec_im = channelize(raw_samples, prototype)
    spectra = jnp.stack([spec_re, spec_im]).astype(jnp.bfloat16)
    spectra = spectra.reshape(2, FINE, INPUTS, DUMPS, MD).transpose(0, 1, 3, 2, 4).reshape(2, FINE * DUMPS, INPUTS, MD)
    block_size = INPUTS // (STN_BLOCKS * CORE_BLOCKS)
    listed = spectra.reshape(2, FINE * DUMPS, STN_BLOCKS, CORE_BLOCKS, block_size, MD)
    listed = listed.transpose(0, 1, 3, 2, 4, 5).reshape(2, FINE * DUMPS, INPUTS, MD)

    def one_slot(slot_data):
        left_rows = jnp.concatenate([slot_data[0], slot_data[1]], axis=1)
        twisted = jnp.concatenate([-slot_data[1], slot_data[0]], axis=1)
        vis_re = jnp.dot(left_rows, left_rows.T, preferred_element_type=jnp.float32)
        vis_im = jnp.dot(left_rows, twisted.T, preferred_element_type=jnp.float32)
        return (jnp.stack([vis_re, vis_im]) * (1.0 / MD)).astype(jnp.bfloat16)

    visibility = lax.map(one_slot, listed.transpose(1, 0, 2, 3))
    real_rows = jnp.concatenate([beam_weight[0], -beam_weight[1]], axis=1)
    imag_rows = jnp.concatenate([beam_weight[1], beam_weight[0]], axis=1)

    def beam_slot(slot_data):
        stacked = jnp.concatenate([slot_data[0], slot_data[1]], axis=0)
        beam_re = jnp.dot(real_rows, stacked, preferred_element_type=jnp.float32)
        beam_im = jnp.dot(imag_rows, stacked, preferred_element_type=jnp.float32)
        return jnp.stack([beam_re, beam_im])

    beam_out = lax.map(beam_slot, spectra.transpose(1, 0, 2, 3)).transpose(1, 0, 2, 3)
    return visibility, beam_out
```

```python
import functools
import math

import jax
import jax.numpy as jnp
from jax import lax
from jax.experimental import pallas as pl
from jax.experimental.pallas import tpu as pltpu
from jax.sharding import PartitionSpec as P

FINE = 16
TAPS = 4
DUMPS = 2
MD = 256
FRAME_TILE = 128
ROW_TILE = 256


def four_point(values):
    (ar, ai), (br, bi), (cr, ci), (dr, di) = values
    sr, si, tr, ti = ar + cr, ai + ci, ar - cr, ai - ci
    ur, ui, vr, vi = br + dr, bi + di, br - dr, bi - di
    return [(sr + ur, si + ui), (tr + vi, ti - vr), (sr - ur, si - ui), (tr - vi, ti + vr)]


def sixteen_point(values):
    half = math.sqrt(0.5)
    columns = []
    for n2 in range(4):
        column = four_point([values[4 * n1 + n2] for n1 in range(4)])
        for k1 in range(1, 4):
            turn = n2 * k1
            re, im = column[k1]
            if turn == 0:
                continue
            if turn == 2:
                column[k1] = ((re + im) * half, (im - re) * half)
            elif turn == 4:
                column[k1] = (im, -re)
            elif turn == 6:
                column[k1] = ((im - re) * half, -(re + im) * half)
            else:
                co, si = math.cos(math.pi * turn / 8), math.sin(math.pi * turn / 8)
                column[k1] = (re * co + im * si, im * co - re * si)
        columns.append(column)
    result = [None] * 16
    for k1 in range(4):
        row = four_point([columns[n2][k1] for n2 in range(4)])
        for k2 in range(4):
            result[k1 + 4 * k2] = row[k2]
    return result


def channel_body(parts, proto_ref, raw_ref, *refs):
    outs, held = refs[:-1], refs[-1]
    for phase in range(FINE):
        for part in range(2):
            total = None
            for tap in range(TAPS):
                rows = raw_ref[part, pl.ds(tap * FINE + phase, FRAME_TILE, stride=FINE), :]
                term = rows * proto_ref[tap * FINE + phase]
                total = term if total is None else total + term
            held[part, phase] = total

    @pl.loop(0, FRAME_TILE // 8)
    def _(step):
        rows = pl.ds(pl.multiple_of(step * 8, 8), 8)
        values = [(held[0, phase, rows, :], held[1, phase, rows, :]) for phase in range(FINE)]
        for channel, (re, im) in enumerate(sixteen_point(values)):
            held[0, channel, rows, :] = re
            held[1, channel, rows, :] = im

    for channel in range(FINE):
        for part in range(2):
            outs[channel % parts][channel // parts, part] = held[part, channel].T.astype(jnp.bfloat16)


def channelize(raw_turned, prototype, dump, parts):
    inputs_here = raw_turned.shape[2]
    tiles = MD // FRAME_TILE
    span = FRAME_TILE * FINE
    block = span + (TAPS - 1) * FINE
    shape = (FINE // parts, 2, inputs_here, MD)
    return pl.pallas_call(
        functools.partial(channel_body, parts),
        grid=(tiles,),
        in_specs=[
            pl.BlockSpec(memory_space=pltpu.SMEM),
            pl.BlockSpec(
                (pl.Element(2), pl.Element(block), pl.Element(inputs_here)),
                lambda i: (0, (dump * tiles + i) * span, 0),
            ),
        ],
        out_specs=[pl.BlockSpec(shape[:3] + (FRAME_TILE,), lambda i: (0, 0, 0, i))] * parts,
        out_shape=[jax.ShapeDtypeStruct(shape, jnp.bfloat16)] * parts,
        scratch_shapes=[pltpu.VMEM((2, FINE, FRAME_TILE, inputs_here), jnp.float32)],
        compiler_params=pltpu.CompilerParams(vmem_limit_bytes=40 * 1024 * 1024),
        cost_estimate=pl.CostEstimate(
            flops=MD * inputs_here * FINE * 40, bytes_accessed=MD * inputs_here * FINE * 12, transcendentals=0
        ),
        name="channelize",
    )(prototype, raw_turned)


def correlate_body(first, half_ref, cols_ref, rows_ref, weight_ref, *refs):
    vis_ref, beam_ref, straight, twisted, sums = refs[-5:]
    step = pl.program_id(0)
    blocks, _, size, _ = cols_ref.shape
    here = rows_ref.shape[0]

    @pl.when(step == 0)
    def _():
        for block in range(blocks):
            span = pl.ds(block * size, size)
            re, im = cols_ref[block, 0], cols_ref[block, 1]
            straight[span, :MD] = re
            straight[span, MD:] = im
            twisted[span, :MD] = -im
            twisted[span, MD:] = re

    re = jnp.concatenate([rows_ref[block, 0] for block in range(here)], axis=0)
    im = jnp.concatenate([rows_ref[block, 1] for block in range(here)], axis=0)
    left = jnp.concatenate([re, im], axis=1)
    contract = (((1,), (1,)), ((), ()))
    for part, right in ((0, straight), (1, twisted)):
        product = lax.dot_general(left, right[...], contract, preferred_element_type=jnp.float32)
        vis_ref[0, part] = (product * (1.0 / MD)).astype(jnp.bfloat16)

    beam_re = beam_im = 0.0
    if size % 128 == 0:
        weights = [
            [jnp.concatenate([weight_ref[block, part] for block in range(here)], axis=1) for part in range(2)]
        ]
        data = [(re, im)]
    else:
        weights = [[weight_ref[block, part] for part in range(2)] for block in range(here)]
        data = [(rows_ref[block, 0], rows_ref[block, 1]) for block in range(here)]
    dot = functools.partial(jnp.dot, preferred_element_type=jnp.float32)
    for (w_re, w_im), (d_re, d_im) in zip(weights, data):
        beam_re += dot(w_re, d_re) - dot(w_im, d_im)
        beam_im += dot(w_im, d_re) + dot(w_re, d_im)

    @pl.when(step == 0)
    def _():
        sums[0] = beam_re if first else beam_re + refs[1][0, 0]
        sums[1] = beam_im if first else beam_im + refs[1][1, 0]

    @pl.when(step > 0)
    def _():
        sums[0] += beam_re
        sums[1] += beam_im

    @pl.when(step == pl.num_programs(0) - 1)
    def _():
        beam_ref[:, 0] = sums[...]


def correlate(half, columns, rows, weights, slot, slots, earlier, first):
    blocks, _, size, _ = columns.shape
    beams = weights.shape[2]
    width = blocks * size
    here = max(1, ROW_TILE // size)
    steps = blocks // here
    tall = here * size
    any_spec = pl.BlockSpec(memory_space=pl.ANY)
    beam_spec = pl.BlockSpec((2, 1, beams, MD), lambda i, half: (0, slot, 0, 0))
    in_specs = [
        pl.BlockSpec(columns.shape, lambda i, half: (0, 0, 0, 0)),
        pl.BlockSpec((here, 2, size, MD), lambda i, half: (i, 0, 0, 0)),
        pl.BlockSpec((here, 2, beams, size), lambda i, half: (i, 0, 0, 0)),
    ]
    operands = [half, columns, rows, weights]
    aliases = {}
    if earlier is not None:
        aliases = {4: 0, 5: 1}
        in_specs += [any_spec, any_spec if first else beam_spec]
        operands += list(earlier)
    return pl.pallas_call(
        functools.partial(correlate_body, first),
        grid_spec=pltpu.PrefetchScalarGridSpec(
            num_scalar_prefetch=1,
            grid=(steps,),
            in_specs=in_specs,
            out_specs=[
                pl.BlockSpec((1, 2, tall, width), lambda i, half: (slot, 0, half[0] * steps + i, 0)),
                beam_spec,
            ],
            scratch_shapes=[
                pltpu.VMEM((width, 2 * MD), jnp.bfloat16),
                pltpu.VMEM((width, 2 * MD), jnp.bfloat16),
                pltpu.VMEM((2, beams, MD), jnp.float32),
            ],
        ),
        out_shape=[
            jax.ShapeDtypeStruct((slots, 2, 2 * width, width), jnp.bfloat16),
            jax.ShapeDtypeStruct((2, slots, beams, MD), jnp.float32),
        ],
        input_output_aliases=aliases,
        compiler_params=pltpu.CompilerParams(vmem_limit_bytes=48 * 1024 * 1024),
        cost_estimate=pl.CostEstimate(
            flops=8 * MD * width * (width + beams), bytes_accessed=5 * width * width, transcendentals=0
        ),
        name="correlate",
    )(*operands)


def per_device(raw_samples, prototype, beam_weight):
    stations = lax.axis_size("stn")
    core = lax.axis_index("tile")
    swap = functools.partial(lax.ppermute, axis_name="tile", perm=[(0, 1), (1, 0)])
    turn = functools.partial(lax.all_to_all, axis_name="stn", split_axis=0, concat_axis=0, tiled=True)
    slots = FINE * DUMPS // stations
    per_dump = max(1, slots // DUMPS)

    raw_turned = raw_samples.transpose(0, 2, 1)
    spectra = [channelize(raw_turned, prototype, dump, per_dump) for dump in range(DUMPS)]
    if slots >= DUMPS:
        chunks = {channel * DUMPS + dump: spectra[dump][channel] for dump in range(DUMPS) for channel in range(per_dump)}
    else:
        both = jnp.stack([spectra[dump][0] for dump in range(DUMPS)], axis=1)
        chunks = {0: both.reshape((stations,) + both.shape[2:])}

    half_beams = beam_weight.shape[1] // 2
    gathered = lax.all_gather(beam_weight, "stn")
    keep = lax.dynamic_slice_in_dim(gathered, core * half_beams, half_beams, 2)
    give = lax.dynamic_slice_in_dim(gathered, (1 - core) * half_beams, half_beams, 2)
    weights = (keep, swap(give))

    outputs = None
    for slot in chunks:
        mine = turn(chunks[slot])
        other = swap(mine)
        for index, rows in enumerate((mine, other)):
            half = (core if index == 0 else 1 - core).astype(jnp.int32).reshape(1)
            outputs = correlate(half, mine, rows, weights[index], slot, slots, outputs, index == 0)
    return tuple(outputs)


def solution(mesh):
    placed = (P(None, ("band", "stn", "tile"), None), P(), P(None, None, ("band", "stn", "tile")))
    return jax.shard_map(
        per_device,
        mesh=mesh,
        in_specs=placed,
        out_specs=(P(("band", "stn"), None, None, "tile"), P(None, ("band", "stn"), "tile", None)),
        check_vma=False,
    )
```

```python
import functools
import math

import jax
import jax.numpy as jnp
from jax import lax
from jax.experimental import pallas as pl
from jax.experimental.pallas import tpu as pltpu
from jax.sharding import PartitionSpec as P

FINE = 16
TAPS = 4
DUMPS = 2
MD = 256
FRAME_TILE = 128
ROW_TILE = 512


def four_point(values):
    (ar, ai), (br, bi), (cr, ci), (dr, di) = values
    sr, si, tr, ti = ar + cr, ai + ci, ar - cr, ai - ci
    ur, ui, vr, vi = br + dr, bi + di, br - dr, bi - di
    return [(sr + ur, si + ui), (tr + vi, ti - vr), (sr - ur, si - ui), (tr - vi, ti + vr)]


def sixteen_point(values):
    half = math.sqrt(0.5)
    columns = []
    for n2 in range(4):
        column = four_point([values[4 * n1 + n2] for n1 in range(4)])
        for k1 in range(1, 4):
            turn = n2 * k1
            re, im = column[k1]
            if turn == 0:
                continue
            if turn == 2:
                column[k1] = ((re + im) * half, (im - re) * half)
            elif turn == 4:
                column[k1] = (im, -re)
            elif turn == 6:
                column[k1] = ((im - re) * half, -(re + im) * half)
            else:
                co, si = math.cos(math.pi * turn / 8), math.sin(math.pi * turn / 8)
                column[k1] = (re * co + im * si, im * co - re * si)
        columns.append(column)
    result = [None] * 16
    for k1 in range(4):
        row = four_point([columns[n2][k1] for n2 in range(4)])
        for k2 in range(4):
            result[k1 + 4 * k2] = row[k2]
    return result


def channel_body(joined, proto_ref, raw_ref, *refs):
    outs, filtered, held = refs[:-2], refs[-2], refs[-1]
    parts = 1 if joined else len(outs)
    halves = FINE // 8
    lane_shape = (8, raw_ref.shape[2])
    place = lax.broadcasted_iota(jnp.int32, lane_shape, 0)

    def column(start):
        values = jnp.full(lane_shape, proto_ref[start])
        for row in range(1, 8):
            values = jnp.where(place == row, proto_ref[start + row], values)
        return values

    taps = [[column(tap * FINE + half * 8) for half in range(halves)] for tap in range(TAPS)]

    @pl.loop(0, FRAME_TILE // 8)
    def _(step):
        base = pl.multiple_of(step * 8 * FINE, 8 * FINE)
        for part in range(2):
            for half in range(halves):
                rows = [raw_ref[part, pl.ds(base + frame * FINE + half * 8, 8), :] for frame in range(8 + TAPS - 1)]
                for frame in range(8):
                    terms = [rows[frame + tap] * taps[tap][half] for tap in range(TAPS)]
                    total = functools.reduce(lambda left, right: left + right, terms)
                    filtered[part, pl.ds(base + frame * FINE + half * 8, 8), :] = total

    @pl.loop(0, FRAME_TILE // 8)
    def _(step):
        base = pl.multiple_of(step * 8 * FINE, 8 * FINE)
        rows = pl.ds(pl.multiple_of(step * 8, 8), 8)
        values = [
            tuple(filtered[part, pl.ds(base + phase, 8, stride=FINE), :] for part in range(2))
            for phase in range(FINE)
        ]
        for channel, (re, im) in enumerate(sixteen_point(values)):
            held[0, channel, rows, :] = re
            held[1, channel, rows, :] = im

    for channel in range(FINE):
        for part in range(2):
            spectrum = held[part, channel].T.astype(jnp.bfloat16)
            if joined:
                each = outs[0].shape[1]
                outs[0][channel // each, channel % each, part] = spectrum
            else:
                outs[channel % parts][channel // parts, 0, part] = spectrum


def channelize(raw_turned, prototype, dump, per_station, joined):
    inputs_here = raw_turned.shape[2]
    tiles = MD // FRAME_TILE
    span = FRAME_TILE * FINE
    block = span + (TAPS - 1) * FINE
    each = per_station if joined else 1
    count = 1 if joined else per_station
    shape = (FINE // per_station, each, 2, inputs_here, MD)
    return pl.pallas_call(
        functools.partial(channel_body, joined),
        grid=(tiles,),
        in_specs=[
            pl.BlockSpec(memory_space=pltpu.SMEM),
            pl.BlockSpec(
                (pl.Element(2), pl.Element(block), pl.Element(inputs_here)),
                lambda i: (0, (dump * tiles + i) * span, 0),
            ),
        ],
        out_specs=[pl.BlockSpec(shape[:4] + (FRAME_TILE,), lambda i: (0, 0, 0, 0, i))] * count,
        scratch_shapes=[
            pltpu.VMEM((2, span, inputs_here), jnp.float32),
            pltpu.VMEM((2, FINE, FRAME_TILE, inputs_here), jnp.float32),
        ],
        out_shape=[jax.ShapeDtypeStruct(shape, jnp.bfloat16)] * count,
        compiler_params=pltpu.CompilerParams(vmem_limit_bytes=60 * 1024 * 1024),
        cost_estimate=pl.CostEstimate(
            flops=MD * inputs_here * FINE * 40, bytes_accessed=MD * inputs_here * FINE * 12, transcendentals=0
        ),
        name="channelize",
    )(prototype, raw_turned)


def correlate_body(cols_ref, other_ref, mine_weight_ref, other_weight_ref, *refs):
    vis_ref, beam_ref, straight, twisted, sums = refs[-5:]
    step = pl.program_id(0)
    steps = pl.num_programs(0) // 2
    blocks, _, size, _ = cols_ref.shape
    here = other_ref.shape[0]
    tall = here * size
    dot = functools.partial(jnp.dot, preferred_element_type=jnp.float32)

    @pl.when(step == 0)
    def _():
        for block in range(blocks):
            span = pl.ds(block * size, size)
            re, im = cols_ref[block, 0], cols_ref[block, 1]
            straight[span, :MD] = re
            straight[span, MD:] = im
            twisted[span, :MD] = -im
            twisted[span, MD:] = re
        sums[...] = jnp.zeros_like(sums)

    def work(left, weight_ref):
        contract = (((1,), (1,)), ((), ()))
        for part, right in ((0, straight), (1, twisted)):
            product = lax.dot_general(left, right[...], contract, preferred_element_type=jnp.float32)
            vis_ref[0, part] = (product * (1.0 / MD)).astype(jnp.bfloat16)
        weights = [[weight_ref[block, part] for part in range(2)] for block in range(here)]
        if size % 128 == 0:
            weights = [[jnp.concatenate([weight[part] for weight in weights], axis=1) for part in range(2)]]
        wide = left.shape[0] // len(weights)
        for block, (w_re, w_im) in enumerate(weights):
            re, im = left[block * wide:(block + 1) * wide, :MD], left[block * wide:(block + 1) * wide, MD:]
            sums[0] += dot(w_re, re) - dot(w_im, im)
            sums[1] += dot(w_im, re) + dot(w_re, im)

    @pl.when(step < steps)
    def _():
        work(straight[pl.ds(pl.multiple_of(step * tall, tall), tall), :], mine_weight_ref)

    @pl.when(step >= steps)
    def _():
        parts = [jnp.concatenate([other_ref[block, part] for block in range(here)], axis=0) for part in range(2)]
        work(jnp.concatenate(parts, axis=1), other_weight_ref)

    @pl.when(step == 2 * steps - 1)
    def _():
        beam_ref[:, 0] = sums[...]


def correlate(core, mine, other, index, weights, slot, slots, earlier):
    blocks, _, _, size, _ = mine.shape
    beams = weights[1].shape[2]
    width = blocks * size
    here = min(blocks, ROW_TILE // size)
    steps = blocks // here

    def clipped(step, half):
        return jnp.maximum(step - steps, 0) if half else jnp.minimum(step, steps - 1)

    in_specs = [
        pl.BlockSpec((blocks, None, 2, size, MD), lambda i, core: (0, index, 0, 0, 0)),
        pl.BlockSpec((here, None, 2, size, MD), lambda i, core: (clipped(i, 1), index, 0, 0, 0)),
        pl.BlockSpec((here, 2, beams, size), lambda i, core: (clipped(i, 0), 0, core[0], 0)),
        pl.BlockSpec((here, 2, beams, size), lambda i, core: (clipped(i, 1), 0, 0, 0)),
    ]
    operands = [core, mine, other, *weights]
    aliases = {}
    if earlier is not None:
        aliases = {5: 0, 6: 1}
        in_specs += [pl.BlockSpec(memory_space=pl.ANY)] * 2
        operands += list(earlier)
    return pl.pallas_call(
        correlate_kernel,
        grid_spec=pltpu.PrefetchScalarGridSpec(
            num_scalar_prefetch=1,
            grid=(2 * steps,),
            in_specs=in_specs,
            out_specs=[
                pl.BlockSpec(
                    (1, 2, here * size, width),
                    lambda i, core: (slot, 0, (core[0] ^ (i // steps)) * steps + i % steps, 0),
                ),
                pl.BlockSpec((2, 1, beams, MD), lambda i, core: (0, slot, 0, 0)),
            ],
            scratch_shapes=[
                pltpu.VMEM((width, 2 * MD), jnp.bfloat16),
                pltpu.VMEM((width, 2 * MD), jnp.bfloat16),
                pltpu.VMEM((2, beams, MD), jnp.float32),
            ],
        ),
        out_shape=[
            jax.ShapeDtypeStruct((slots, 2, 2 * width, width), jnp.bfloat16),
            jax.ShapeDtypeStruct((2, slots, beams, MD), jnp.float32),
        ],
        input_output_aliases=aliases,
        compiler_params=pltpu.CompilerParams(vmem_limit_bytes=60 * 1024 * 1024),
        cost_estimate=pl.CostEstimate(
            flops=16 * MD * width * (width + beams), bytes_accessed=10 * width * width, transcendentals=0
        ),
        name="correlate",
    )(*operands)


def correlate_kernel(core_ref, *refs):
    correlate_body(*refs)


def exchange(values, axis, turn):
    count = lax.axis_size(axis)
    return lax.ppermute(values, axis, [(index, index ^ turn) for index in range(count)])


def per_device(raw_samples, prototype, beam_weight):
    stations = lax.axis_size("stn")
    core = lax.axis_index("tile")
    slots = FINE * DUMPS // stations
    per_dump = max(1, slots // DUMPS)
    turn = functools.partial(lax.all_to_all, axis_name="stn", split_axis=0, concat_axis=0, tiled=True)

    raw_turned = raw_samples.transpose(0, 2, 1)
    spectra = [channelize(raw_turned, prototype, dump, per_dump, dump == 0) for dump in range(DUMPS)]
    if slots >= DUMPS:
        chunks = [(part, [DUMPS * index for index in range(per_dump)]) for part in spectra[0]]
        chunks += [(part, [DUMPS * index + 1]) for index, part in enumerate(spectra[1])]
    else:
        whole = jnp.stack([spectra[dump][0] for dump in range(DUMPS)], axis=1)
        chunks = [(whole.reshape((stations,) + whole.shape[2:]), [0])]

    half_beams = beam_weight.shape[1] // 2
    gathered = lax.all_gather(beam_weight, "stn")
    give = lax.dynamic_slice_in_dim(gathered, (1 - core) * half_beams, half_beams, 2)
    weights = (gathered, exchange(give, "tile", 1))
    where = core.astype(jnp.int32).reshape(1)

    outputs = None
    before = [chunk for chunk, _ in chunks[1:]]
    arrived = turn(chunks[0][0])
    for number, (_, held) in enumerate(chunks):
        mine, before = lax.optimization_barrier((arrived, before))
        if number + 1 < len(chunks):
            arrived = turn(chunks[number + 1][0] if number else before[0])
        other = exchange(mine, "tile", 1)
        for index, slot in enumerate(held):
            outputs = correlate(where, mine, other, index, weights, slot, slots, outputs)
        outputs = before = lax.optimization_barrier(tuple(outputs))
    return tuple(outputs)


def solution(mesh):
    placed = (P(None, ("band", "stn", "tile"), None), P(), P(None, None, ("band", "stn", "tile")))
    return jax.shard_map(
        per_device,
        mesh=mesh,
        in_specs=placed,
        out_specs=(P(("band", "stn"), None, None, "tile"), P(None, ("band", "stn"), "tile", None)),
        check_vma=False,
    )
```

```python
import functools
import math

import jax
import jax.numpy as jnp
from jax import lax
from jax.experimental import pallas as pl
from jax.experimental.pallas import tpu as pltpu
from jax.sharding import PartitionSpec as P

FINE = 16
TAPS = 4
DUMPS = 2
MD = 256
FRAME_TILE = 128
ROW_TILE = 512
VMEM_LIMIT = 64 * 1024 * 1024


def four_point(values):
    (ar, ai), (br, bi), (cr, ci), (dr, di) = values
    sr, si, tr, ti = ar + cr, ai + ci, ar - cr, ai - ci
    ur, ui, vr, vi = br + dr, bi + di, br - dr, bi - di
    return [(sr + ur, si + ui), (tr + vi, ti - vr), (sr - ur, si - ui), (tr - vi, ti + vr)]


def sixteen_point(values):
    half = math.sqrt(0.5)
    columns = []
    for n2 in range(4):
        column = four_point([values[4 * n1 + n2] for n1 in range(4)])
        for k1 in range(1, 4):
            turn = n2 * k1
            re, im = column[k1]
            if turn == 0:
                continue
            if turn == 2:
                column[k1] = ((re + im) * half, (im - re) * half)
            elif turn == 4:
                column[k1] = (im, -re)
            elif turn == 6:
                column[k1] = ((im - re) * half, -(re + im) * half)
            else:
                co, si = math.cos(math.pi * turn / 8), math.sin(math.pi * turn / 8)
                column[k1] = (re * co + im * si, im * co - re * si)
        columns.append(column)
    result = [None] * 16
    for k1 in range(4):
        row = four_point([columns[n2][k1] for n2 in range(4)])
        for k2 in range(4):
            result[k1 + 4 * k2] = row[k2]
    return result


def channel_body(joined, proto_ref, raw_ref, *refs):
    outs, filtered, held = refs[:-2], refs[-2], refs[-1]
    parts = 1 if joined else len(outs)
    halves = FINE // 8
    lane_shape = (8, raw_ref.shape[2])
    place = lax.broadcasted_iota(jnp.int32, lane_shape, 0)

    def column(start):
        values = jnp.full(lane_shape, proto_ref[start])
        for row in range(1, 8):
            values = jnp.where(place == row, proto_ref[start + row], values)
        return values

    taps = [[column(tap * FINE + half * 8) for half in range(halves)] for tap in range(TAPS)]

    @pl.loop(0, FRAME_TILE // 8)
    def _(step):
        base = pl.multiple_of(step * 8 * FINE, 8 * FINE)
        for part in range(2):
            for half in range(halves):
                rows = [raw_ref[part, pl.ds(base + frame * FINE + half * 8, 8), :] for frame in range(8 + TAPS - 1)]
                for frame in range(8):
                    terms = [rows[frame + tap] * taps[tap][half] for tap in range(TAPS)]
                    total = functools.reduce(lambda left, right: left + right, terms)
                    filtered[part, pl.ds(base + frame * FINE + half * 8, 8), :] = total

    @pl.loop(0, FRAME_TILE // 8)
    def _(step):
        base = pl.multiple_of(step * 8 * FINE, 8 * FINE)
        rows = pl.ds(pl.multiple_of(step * 8, 8), 8)
        values = [
            tuple(filtered[part, pl.ds(base + phase, 8, stride=FINE), :] for part in range(2))
            for phase in range(FINE)
        ]
        for channel, (re, im) in enumerate(sixteen_point(values)):
            held[0, channel, rows, :] = re
            held[1, channel, rows, :] = im

    for channel in range(FINE):
        for part in range(2):
            spectrum = held[part, channel].T.astype(jnp.bfloat16)
            if joined:
                each = outs[0].shape[1]
                outs[0][channel // each, channel % each, part] = spectrum
            else:
                outs[channel % parts][channel // parts, 0, part] = spectrum


def channelize(raw_turned, prototype, dump, per_station, joined):
    inputs_here = raw_turned.shape[2]
    tiles = MD // FRAME_TILE
    span = FRAME_TILE * FINE
    block = span + (TAPS - 1) * FINE
    each = per_station if joined else 1
    count = 1 if joined else per_station
    shape = (FINE // per_station, each, 2, inputs_here, MD)
    return pl.pallas_call(
        functools.partial(channel_body, joined),
        grid=(tiles,),
        in_specs=[
            pl.BlockSpec(memory_space=pltpu.SMEM),
            pl.BlockSpec(
                (pl.Element(2), pl.Element(block), pl.Element(inputs_here)),
                lambda i: (0, (dump * tiles + i) * span, 0),
            ),
        ],
        out_specs=[pl.BlockSpec(shape[:4] + (FRAME_TILE,), lambda i: (0, 0, 0, 0, i))] * count,
        scratch_shapes=[
            pltpu.VMEM((2, span, inputs_here), jnp.float32),
            pltpu.VMEM((2, FINE, FRAME_TILE, inputs_here), jnp.float32),
        ],
        out_shape=[jax.ShapeDtypeStruct(shape, jnp.bfloat16)] * count,
        compiler_params=pltpu.CompilerParams(vmem_limit_bytes=VMEM_LIMIT),
        cost_estimate=pl.CostEstimate(
            flops=MD * inputs_here * FINE * 40, bytes_accessed=MD * inputs_here * FINE * 12, transcendentals=0
        ),
        name="channelize",
    )(prototype, raw_turned)


def add_beams(sums, rows, order, weight_ref):
    dot = functools.partial(jnp.dot, preferred_element_type=jnp.float32)
    weights = [[weight_ref[high, low, part] for part in range(2)] for high, low in order]
    if weight_ref.shape[4] % 128 == 0:
        weights = [[jnp.concatenate([weight[part] for weight in weights], axis=1) for part in range(2)]]
    wide = rows.shape[0] // len(weights)
    for block, (w_re, w_im) in enumerate(weights):
        re, im = rows[block * wide:(block + 1) * wide, :MD], rows[block * wide:(block + 1) * wide, MD:]
        sums[0] += dot(w_re, re) - dot(w_im, im)
        sums[1] += dot(w_im, re) + dot(w_re, im)


def beams_body(where_ref, mine_ref, other_ref, mine_weight_ref, other_weight_ref, *refs):
    beam_ref, sums = refs[-2:]
    blocks = mine_ref.shape[0]
    inner = mine_weight_ref.shape[1]
    order = [((block ^ where_ref[1]) // inner, (block ^ where_ref[1]) % inner) for block in range(blocks)]
    sums[...] = jnp.zeros_like(sums)
    for rows_ref, weight_ref in ((mine_ref, mine_weight_ref), (other_ref, other_weight_ref)):
        parts = [jnp.concatenate([rows_ref[block, part] for block in range(blocks)], axis=0) for part in range(2)]
        add_beams(sums, jnp.concatenate(parts, axis=1), order, weight_ref)
    beam_ref[:, 0] = sums[...]


def form_beams(where, mine, other, weights, held, earlier):
    blocks, count, _, size, _ = mine.shape
    outer, inner, _, beams, _ = weights[1].shape
    rows_spec = pl.BlockSpec((blocks, None, 2, size, MD), lambda i, where: (0, i, 0, 0, 0))
    stride = held[1] - held[0] if count > 1 else 0
    return pl.pallas_call(
        beams_body,
        grid_spec=pltpu.PrefetchScalarGridSpec(
            num_scalar_prefetch=1,
            grid=(count,),
            in_specs=[
                rows_spec,
                rows_spec,
                pl.BlockSpec((outer, inner, 2, beams, size), lambda i, where: (0, 0, 0, where[0], 0)),
                pl.BlockSpec((outer, inner, 2, beams, size), lambda i, where: (0, 0, 0, 0, 0)),
                pl.BlockSpec(memory_space=pl.ANY),
            ],
            out_specs=pl.BlockSpec((2, 1, beams, MD), lambda i, where: (0, held[0] + i * stride, 0, 0)),
            scratch_shapes=[pltpu.VMEM((2, beams, MD), jnp.float32)],
        ),
        out_shape=jax.ShapeDtypeStruct(earlier.shape, earlier.dtype),
        input_output_aliases={5: 0},
        compiler_params=pltpu.CompilerParams(vmem_limit_bytes=VMEM_LIMIT),
        cost_estimate=pl.CostEstimate(
            flops=count * 16 * MD * blocks * size * beams, bytes_accessed=count * 8 * MD * blocks * size, transcendentals=0
        ),
        name="form_beams",
    )(where, mine, other, *weights, earlier)


def correlate_body(with_beams, where_ref, cols_ref, other_ref, *refs):
    mine_weight_ref, other_weight_ref = refs[:2] if with_beams else (None, None)
    vis_ref, straight, twisted = refs[-5], refs[-2], refs[-1]
    beam_ref, sums = refs[-4], refs[-3]
    place = where_ref[1]
    step = pl.program_id(0)
    steps = pl.num_programs(0) // 2
    blocks, _, size, _ = cols_ref.shape
    here = other_ref.shape[0]
    tall = here * size

    @pl.when(step == 0)
    def _():
        for block in range(blocks):
            span = pl.ds(block * size, size)
            re, im = cols_ref[block, 0], cols_ref[block, 1]
            straight[span, :MD] = re
            straight[span, MD:] = im
            twisted[span, :MD] = -im
            twisted[span, MD:] = re
        if with_beams:
            sums[...] = jnp.zeros_like(sums)

    def work(left, weight_ref):
        contract = (((1,), (1,)), ((), ()))
        for part, right in ((0, straight), (1, twisted)):
            product = lax.dot_general(left, right[...], contract, preferred_element_type=jnp.float32)
            vis_ref[0, part] = (product * (1.0 / MD)).astype(jnp.bfloat16)
        if with_beams:
            inner = weight_ref.shape[1]
            add_beams(sums, left, [((block // inner) ^ ((place // inner) % (here // inner)), (block ^ place) % inner) for block in range(here)], weight_ref)

    @pl.when(step < steps)
    def _():
        work(straight[pl.ds(pl.multiple_of(step * tall, tall), tall), :], mine_weight_ref)

    @pl.when(step >= steps)
    def _():
        parts = [jnp.concatenate([other_ref[block, part] for block in range(here)], axis=0) for part in range(2)]
        work(jnp.concatenate(parts, axis=1), other_weight_ref)

    if with_beams:
        @pl.when(step == 2 * steps - 1)
        def _():
            beam_ref[:, 0] = sums[...]


def correlate(where, mine, other, index, weights, slot, slots, beams, earlier):
    blocks, _, _, size, _ = mine.shape
    width = blocks * size
    here = min(blocks, ROW_TILE // size)
    steps = blocks // here
    beam_shape = (2, slots, beams, MD)

    def clipped(step, half):
        return jnp.maximum(step - steps, 0) if half else jnp.minimum(step, steps - 1)

    in_specs = [
        pl.BlockSpec((blocks, None, 2, size, MD), lambda i, where: (0, index, 0, 0, 0)),
        pl.BlockSpec((here, None, 2, size, MD), lambda i, where: (clipped(i, 1), index, 0, 0, 0)),
    ]
    operands = [where, mine, other]
    if weights is not None:
        inner = weights[0].shape[1]
        weight_block = (here // inner, inner, 2, beams, size)
        in_specs += [
            pl.BlockSpec(weight_block, lambda i, where: (clipped(i, 0) ^ (where[1] // here), 0, 0, where[0], 0)),
            pl.BlockSpec(weight_block, lambda i, where: (clipped(i, 1) ^ (where[1] // here), 0, 0, 0, 0)),
        ]
        operands += list(weights)
        beam_spec = pl.BlockSpec((2, 1, beams, MD), lambda i, where: (0, slot, 0, 0))
    else:
        beam_spec = pl.BlockSpec(memory_space=pl.ANY)
    aliases = {}
    if earlier is not None:
        aliases = {len(operands): 0, len(operands) + 1: 1}
        in_specs += [pl.BlockSpec(memory_space=pl.ANY)] * 2
        operands += list(earlier)
    return pl.pallas_call(
        functools.partial(correlate_body, weights is not None),
        grid_spec=pltpu.PrefetchScalarGridSpec(
            num_scalar_prefetch=1,
            grid=(2 * steps,),
            in_specs=in_specs,
            out_specs=[
                pl.BlockSpec(
                    (1, 2, here * size, width),
                    lambda i, where: (slot, 0, (where[0] ^ (i // steps)) * steps + i % steps, 0),
                ),
                beam_spec,
            ],
            scratch_shapes=[
                pltpu.VMEM((2, beams, MD) if weights is not None else (8, 128), jnp.float32),
                pltpu.VMEM((width, 2 * MD), jnp.bfloat16),
                pltpu.VMEM((width, 2 * MD), jnp.bfloat16),
            ],
        ),
        out_shape=[
            jax.ShapeDtypeStruct((slots, 2, 2 * width, width), jnp.bfloat16),
            jax.ShapeDtypeStruct(beam_shape, jnp.float32),
        ],
        input_output_aliases=aliases,
        compiler_params=pltpu.CompilerParams(vmem_limit_bytes=VMEM_LIMIT),
        cost_estimate=pl.CostEstimate(
            flops=16 * MD * width * width, bytes_accessed=10 * width * width, transcendentals=0
        ),
        name="correlate",
    )(*operands)


def exchange(values, axis, turn):
    count = lax.axis_size(axis)
    return lax.ppermute(values, axis, [(index, index ^ turn) for index in range(count)])


def spread_start(weight, ready, inner):
    stations = lax.axis_size("stn")
    outer = stations // inner
    if outer != 4:
        place = lax.axis_index("stn")
        gathered = jnp.take(lax.all_gather(weight, "stn"), place ^ jnp.arange(stations), axis=0)
        return gathered.reshape((outer, inner) + weight.shape), ready
    opposite, ready = lax.optimization_barrier((exchange(weight, "stn", 3 * inner), ready))
    pair = jnp.stack([weight, opposite])
    return (pair, exchange(pair, "stn", 1), exchange(pair, "stn", inner)), ready


def spread_middle(held, inner):
    if not isinstance(held, tuple):
        return held
    return held + (exchange(held[2], "stn", 1),)


def spread_finish(held):
    if not isinstance(held, tuple):
        return held
    pair, beside, side, across = held
    return jnp.stack(
        [
            jnp.stack([pair[0], beside[0]]),
            jnp.stack([side[0], across[0]]),
            jnp.stack([side[1], across[1]]),
            jnp.stack([pair[1], beside[1]]),
        ]
    )


def per_device(raw_samples, prototype, beam_weight):
    stations = lax.axis_size("stn")
    core = lax.axis_index("tile")
    inner = 2
    slots = FINE * DUMPS // stations
    per_dump = max(1, slots // DUMPS)
    turn = functools.partial(lax.all_to_all, axis_name="stn", split_axis=0, concat_axis=0, tiled=True)

    raw_turned = raw_samples.transpose(0, 2, 1)
    spectra = [channelize(raw_turned, prototype, dump, per_dump, dump == 0) for dump in range(DUMPS)]
    if slots >= DUMPS:
        chunks = [(part, [DUMPS * index for index in range(per_dump)]) for part in spectra[0]]
        chunks += [(part, [DUMPS * index + 1]) for index, part in enumerate(spectra[1])]
    else:
        whole = jnp.stack([spectra[dump][0] for dump in range(DUMPS)], axis=1)
        chunks = [(whole.reshape((stations,) + whole.shape[2:]), [0])]

    half_beams = beam_weight.shape[1] // 2
    where = jnp.stack([core, lax.axis_index("stn")]).astype(jnp.int32)
    spread, first = spread_start(beam_weight, chunks[0][0], inner)

    outputs = weights = None
    waiting = []
    before = [chunk for chunk, _ in chunks[1:]]
    arrived = turn(first)
    for number, (_, held) in enumerate(chunks):
        final = number + 1 == len(chunks)
        if weights is None:
            mine, before, spread = lax.optimization_barrier((arrived, before, spread))
            if number == 0:
                spread = spread_middle(spread, inner)
        else:
            mine, before = lax.optimization_barrier((arrived, before))
        if not final:
            arrived = turn(chunks[number + 1][0] if number else before[0])
        other = exchange(mine, "tile", 1)
        if weights is None and (number == 1 or final):
            spread = spread_finish(spread)
            give = lax.dynamic_slice_in_dim(spread, (1 - core) * half_beams, half_beams, 3)
            weights = (spread, exchange(give, "tile", 1))
        for index, slot in enumerate(held):
            fused = weights if final else None
            outputs = correlate(where, mine, other, index, fused, slot, slots, half_beams, outputs)
        if not final:
            waiting.append((mine, other, held))
        if weights is not None:
            for earlier_mine, earlier_other, earlier_held in waiting:
                beams = form_beams(where, earlier_mine, earlier_other, weights, earlier_held, outputs[1])
                outputs = (outputs[0], beams)
            waiting = []
        outputs = before = lax.optimization_barrier(tuple(outputs))
    return tuple(outputs)


def solution(mesh):
    placed = (P(None, ("band", "stn", "tile"), None), P(), P(None, None, ("band", "stn", "tile")))
    return jax.shard_map(
        per_device,
        mesh=mesh,
        in_specs=placed,
        out_specs=(P(("band", "stn"), None, None, "tile"), P(None, ("band", "stn"), "tile", None)),
        check_vma=False,
    )
```

```python
import functools
import math

import jax
import jax.numpy as jnp
from jax import lax
from jax.experimental import pallas as pl
from jax.experimental.pallas import tpu as pltpu
from jax.sharding import PartitionSpec as P

FINE = 16
TAPS = 4
DUMPS = 2
MD = 256
FRAME_TILE = 128
ROW_TILE = 512
VMEM_LIMIT = 64 * 1024 * 1024


def four_point(values):
    (ar, ai), (br, bi), (cr, ci), (dr, di) = values
    sr, si, tr, ti = ar + cr, ai + ci, ar - cr, ai - ci
    ur, ui, vr, vi = br + dr, bi + di, br - dr, bi - di
    return [(sr + ur, si + ui), (tr + vi, ti - vr), (sr - ur, si - ui), (tr - vi, ti + vr)]


def sixteen_point(values):
    half = math.sqrt(0.5)
    columns = []
    for n2 in range(4):
        column = four_point([values[4 * n1 + n2] for n1 in range(4)])
        for k1 in range(1, 4):
            turn = n2 * k1
            re, im = column[k1]
            if turn == 0:
                continue
            if turn == 2:
                column[k1] = ((re + im) * half, (im - re) * half)
            elif turn == 4:
                column[k1] = (im, -re)
            elif turn == 6:
                column[k1] = ((im - re) * half, -(re + im) * half)
            else:
                co, si = math.cos(math.pi * turn / 8), math.sin(math.pi * turn / 8)
                column[k1] = (re * co + im * si, im * co - re * si)
        columns.append(column)
    result = [None] * 16
    for k1 in range(4):
        row = four_point([columns[n2][k1] for n2 in range(4)])
        for k2 in range(4):
            result[k1 + 4 * k2] = row[k2]
    return result


def channel_body(joined, proto_ref, raw_ref, *refs):
    outs, filtered, held = refs[:-2], refs[-2], refs[-1]
    parts = 1 if joined else len(outs)
    halves = FINE // 8
    lane_shape = (8, raw_ref.shape[2])
    place = lax.broadcasted_iota(jnp.int32, lane_shape, 0)

    def column(start):
        values = jnp.full(lane_shape, proto_ref[start])
        for row in range(1, 8):
            values = jnp.where(place == row, proto_ref[start + row], values)
        return values

    taps = [[column(tap * FINE + half * 8) for half in range(halves)] for tap in range(TAPS)]

    @pl.loop(0, FRAME_TILE // 8)
    def _(step):
        base = pl.multiple_of(step * 8 * FINE, 8 * FINE)
        for part in range(2):
            for half in range(halves):
                rows = [raw_ref[part, pl.ds(base + frame * FINE + half * 8, 8), :] for frame in range(8 + TAPS - 1)]
                for frame in range(8):
                    terms = [rows[frame + tap] * taps[tap][half] for tap in range(TAPS)]
                    total = functools.reduce(lambda left, right: left + right, terms)
                    filtered[part, pl.ds(base + frame * FINE + half * 8, 8), :] = total

    @pl.loop(0, FRAME_TILE // 8)
    def _(step):
        base = pl.multiple_of(step * 8 * FINE, 8 * FINE)
        rows = pl.ds(pl.multiple_of(step * 8, 8), 8)
        values = [
            tuple(filtered[part, pl.ds(base + phase, 8, stride=FINE), :] for part in range(2))
            for phase in range(FINE)
        ]
        for channel, (re, im) in enumerate(sixteen_point(values)):
            held[0, channel, rows, :] = re
            held[1, channel, rows, :] = im

    for channel in range(FINE):
        for part in range(2):
            spectrum = held[part, channel].T.astype(jnp.bfloat16)
            if joined:
                each = outs[0].shape[1]
                outs[0][channel // each, channel % each, part] = spectrum
            else:
                outs[channel % parts][channel // parts, 0, part] = spectrum


def channelize(raw_turned, prototype, dump, per_station, joined):
    inputs_here = raw_turned.shape[2]
    tiles = MD // FRAME_TILE
    span = FRAME_TILE * FINE
    block = span + (TAPS - 1) * FINE
    each = per_station if joined else 1
    count = 1 if joined else per_station
    shape = (FINE // per_station, each, 2, inputs_here, MD)
    return pl.pallas_call(
        functools.partial(channel_body, joined),
        grid=(tiles,),
        in_specs=[
            pl.BlockSpec(memory_space=pltpu.SMEM),
            pl.BlockSpec(
                (pl.Element(2), pl.Element(block), pl.Element(inputs_here)),
                lambda i: (0, (dump * tiles + i) * span, 0),
            ),
        ],
        out_specs=[pl.BlockSpec(shape[:4] + (FRAME_TILE,), lambda i: (0, 0, 0, 0, i))] * count,
        scratch_shapes=[
            pltpu.VMEM((2, span, inputs_here), jnp.float32),
            pltpu.VMEM((2, FINE, FRAME_TILE, inputs_here), jnp.float32),
        ],
        out_shape=[jax.ShapeDtypeStruct(shape, jnp.bfloat16)] * count,
        compiler_params=pltpu.CompilerParams(vmem_limit_bytes=VMEM_LIMIT),
        cost_estimate=pl.CostEstimate(
            flops=MD * inputs_here * FINE * (40 if dump == 0 else 400000),
            bytes_accessed=MD * inputs_here * FINE * 12,
            transcendentals=0,
        ),
        name="channelize",
    )(prototype, raw_turned)


def add_beams(sums, rows, order, weight_ref):
    beams, size = weight_ref.shape[3:]
    weights = [jnp.concatenate([weight_ref[high, low, 0], weight_ref[high, low, 1]], axis=0) for high, low in order]
    if size % 128 == 0:
        weights = [jnp.concatenate(weights, axis=1)]
    wide = rows.shape[0] // len(weights)
    for block, weight in enumerate(weights):
        product = jnp.dot(weight, rows[block * wide:(block + 1) * wide], preferred_element_type=jnp.float32)
        sums[0] += product[:beams, :MD] - product[beams:, MD:]
        sums[1] += product[beams:, :MD] + product[:beams, MD:]


def beams_body(counts, where_ref, mine_weight_ref, other_weight_ref, *refs):
    beam_ref, sums = refs[-2:]
    step = pl.program_id(0)
    inner = mine_weight_ref.shape[1]
    sums[...] = jnp.zeros_like(sums)

    def work(mine_ref, other_ref):
        blocks = mine_ref.shape[0]
        order = [((block ^ where_ref[1]) // inner, (block ^ where_ref[1]) % inner) for block in range(blocks)]
        for rows_ref, weight_ref in ((mine_ref, mine_weight_ref), (other_ref, other_weight_ref)):
            parts = [jnp.concatenate([rows_ref[block, part] for block in range(blocks)], axis=0) for part in range(2)]
            add_beams(sums, jnp.concatenate(parts, axis=1), order, weight_ref)

    start = 0
    for group, count in enumerate(counts):
        @pl.when((step >= start) & (step < start + count))
        def _(group=group):
            work(refs[2 * group], refs[2 * group + 1])

        start += count
    beam_ref[:, 0] = sums[...]


def form_beams(where, groups, weights, earlier):
    blocks, _, _, size, _ = groups[0][0].shape
    outer, inner, _, beams, _ = weights[1].shape
    counts = [len(held) for _, _, held in groups]
    held = [slot for _, _, slots in groups for slot in slots]
    weight_block = (outer, inner, 2, beams, size)
    in_specs = [
        pl.BlockSpec(weight_block, lambda i, where: (0, 0, 0, where[0], 0)),
        pl.BlockSpec(weight_block, lambda i, where: (0, 0, 0, 0, 0)),
    ]
    operands = [where, *weights]
    for group, (mine, other, _) in enumerate(groups):
        start, count = sum(counts[:group]), counts[group]

        def picked(i, where, start=start, count=count):
            return (0, jnp.clip(i - start, 0, count - 1), 0, 0, 0)

        in_specs += [pl.BlockSpec((blocks, None, 2, size, MD), picked)] * 2
        operands += [mine, other]

    def target(i, where):
        return (0, sum(jnp.where(i == step, slot, 0) for step, slot in enumerate(held)), 0, 0)

    return pl.pallas_call(
        functools.partial(beams_body, counts),
        grid_spec=pltpu.PrefetchScalarGridSpec(
            num_scalar_prefetch=1,
            grid=(len(held),),
            in_specs=in_specs + [pl.BlockSpec(memory_space=pl.ANY)],
            out_specs=pl.BlockSpec((2, 1, beams, MD), target),
            scratch_shapes=[pltpu.VMEM((2, beams, MD), jnp.float32)],
        ),
        out_shape=jax.ShapeDtypeStruct(earlier.shape, earlier.dtype),
        input_output_aliases={len(operands): 0},
        compiler_params=pltpu.CompilerParams(vmem_limit_bytes=VMEM_LIMIT),
        cost_estimate=pl.CostEstimate(
            flops=len(held) * 16 * MD * blocks * size * beams,
            bytes_accessed=len(held) * 8 * MD * blocks * size,
            transcendentals=0,
        ),
        name="form_beams",
    )(*operands, earlier)


def correlate_body(with_beams, where_ref, cols_ref, other_ref, *refs):
    mine_weight_ref, other_weight_ref = refs[:2] if with_beams else (None, None)
    vis_ref, straight, twisted = refs[-5], refs[-2], refs[-1]
    beam_ref, sums = refs[-4], refs[-3]
    place = where_ref[1]
    step = pl.program_id(0)
    steps = pl.num_programs(0) // 2
    blocks, _, size, _ = cols_ref.shape
    here = other_ref.shape[0]
    tall = here * size

    @pl.when(step == 0)
    def _():
        for block in range(blocks):
            span = pl.ds(block * size, size)
            re, im = cols_ref[block, 0], cols_ref[block, 1]
            straight[span, :MD] = re
            straight[span, MD:] = im
            twisted[span, :MD] = -im
            twisted[span, MD:] = re
        if with_beams:
            sums[...] = jnp.zeros_like(sums)

    def work(left, weight_ref):
        contract = (((1,), (1,)), ((), ()))
        for part, right in ((0, straight), (1, twisted)):
            product = lax.dot_general(left, right[...], contract, preferred_element_type=jnp.float32)
            vis_ref[0, part] = (product * (1.0 / MD)).astype(jnp.bfloat16)
        if with_beams:
            inner = weight_ref.shape[1]
            add_beams(sums, left, [((block // inner) ^ ((place // inner) % (here // inner)), (block ^ place) % inner) for block in range(here)], weight_ref)

    @pl.when(step < steps)
    def _():
        work(straight[pl.ds(pl.multiple_of(step * tall, tall), tall), :], mine_weight_ref)

    @pl.when(step >= steps)
    def _():
        parts = [jnp.concatenate([other_ref[block, part] for block in range(here)], axis=0) for part in range(2)]
        work(jnp.concatenate(parts, axis=1), other_weight_ref)

    if with_beams:
        @pl.when(step == 2 * steps - 1)
        def _():
            beam_ref[:, 0] = sums[...]


def correlate(where, mine, other, index, weights, slot, slots, beams, earlier):
    blocks, _, _, size, _ = mine.shape
    width = blocks * size
    here = min(blocks, ROW_TILE // size)
    steps = blocks // here
    beam_shape = (2, slots, beams, MD)

    def clipped(step, half):
        return jnp.maximum(step - steps, 0) if half else jnp.minimum(step, steps - 1)

    in_specs = [
        pl.BlockSpec((blocks, None, 2, size, MD), lambda i, where: (0, index, 0, 0, 0)),
        pl.BlockSpec((here, None, 2, size, MD), lambda i, where: (clipped(i, 1), index, 0, 0, 0)),
    ]
    operands = [where, mine, other]
    if weights is not None:
        inner = weights[0].shape[1]
        weight_block = (here // inner, inner, 2, beams, size)
        in_specs += [
            pl.BlockSpec(weight_block, lambda i, where: (clipped(i, 0) ^ (where[1] // here), 0, 0, where[0], 0)),
            pl.BlockSpec(weight_block, lambda i, where: (clipped(i, 1) ^ (where[1] // here), 0, 0, 0, 0)),
        ]
        operands += list(weights)
        beam_spec = pl.BlockSpec((2, 1, beams, MD), lambda i, where: (0, slot, 0, 0))
    else:
        beam_spec = pl.BlockSpec(memory_space=pl.ANY)
    aliases = {}
    if earlier is not None:
        aliases = {len(operands): 0, len(operands) + 1: 1}
        in_specs += [pl.BlockSpec(memory_space=pl.ANY)] * 2
        operands += list(earlier)
    return pl.pallas_call(
        functools.partial(correlate_body, weights is not None),
        grid_spec=pltpu.PrefetchScalarGridSpec(
            num_scalar_prefetch=1,
            grid=(2 * steps,),
            in_specs=in_specs,
            out_specs=[
                pl.BlockSpec(
                    (1, 2, here * size, width),
                    lambda i, where: (slot, 0, (where[0] ^ (i // steps)) * steps + i % steps, 0),
                ),
                beam_spec,
            ],
            scratch_shapes=[
                pltpu.VMEM((2, beams, MD) if weights is not None else (8, 128), jnp.float32),
                pltpu.VMEM((width, 2 * MD), jnp.bfloat16),
                pltpu.VMEM((width, 2 * MD), jnp.bfloat16),
            ],
        ),
        out_shape=[
            jax.ShapeDtypeStruct((slots, 2, 2 * width, width), jnp.bfloat16),
            jax.ShapeDtypeStruct(beam_shape, jnp.float32),
        ],
        input_output_aliases=aliases,
        compiler_params=pltpu.CompilerParams(vmem_limit_bytes=VMEM_LIMIT),
        cost_estimate=pl.CostEstimate(
            flops=16 * MD * width * width, bytes_accessed=10 * width * width, transcendentals=0
        ),
        name="correlate",
    )(*operands)


def exchange(values, axis, turn):
    count = lax.axis_size(axis)
    return lax.ppermute(values, axis, [(index, index ^ turn) for index in range(count)])


def spread_start(weight, ready, inner):
    stations = lax.axis_size("stn")
    outer = stations // inner
    if outer != 4:
        place = lax.axis_index("stn")
        gathered = jnp.take(lax.all_gather(weight, "stn"), place ^ jnp.arange(stations), axis=0)
        return gathered.reshape((outer, inner) + weight.shape), ready
    opposite, ready = lax.optimization_barrier((exchange(weight, "stn", 3 * inner), ready))
    pair = jnp.stack([weight, opposite])
    return (pair, exchange(pair, "stn", 1), exchange(pair, "stn", inner)), ready


def spread_middle(held, inner):
    if not isinstance(held, tuple):
        return held
    return held + (exchange(held[2], "stn", 1),)


def spread_finish(held):
    if not isinstance(held, tuple):
        return held
    pair, beside, side, across = held
    return jnp.stack(
        [
            jnp.stack([pair[0], beside[0]]),
            jnp.stack([side[0], across[0]]),
            jnp.stack([side[1], across[1]]),
            jnp.stack([pair[1], beside[1]]),
        ]
    )


def per_device(raw_samples, prototype, beam_weight):
    stations = lax.axis_size("stn")
    core = lax.axis_index("tile")
    inner = 2
    slots = FINE * DUMPS // stations
    per_dump = max(1, slots // DUMPS)
    turn = functools.partial(lax.all_to_all, axis_name="stn", split_axis=0, concat_axis=0, tiled=True)

    raw_turned = raw_samples.transpose(0, 2, 1)
    spectra = [channelize(raw_turned, prototype, 0, per_dump, True)]
    spread, raw_turned = spread_start(beam_weight, raw_turned, inner)
    spectra += [channelize(raw_turned, prototype, dump, per_dump, False) for dump in range(1, DUMPS)]
    if slots >= DUMPS:
        chunks = [(part, [DUMPS * index for index in range(per_dump)]) for part in spectra[0]]
        chunks += [(part, [DUMPS * index + 1]) for index, part in enumerate(spectra[1])]
    else:
        whole = jnp.stack([spectra[dump][0] for dump in range(DUMPS)], axis=1)
        chunks = [(whole.reshape((stations,) + whole.shape[2:]), [0])]

    half_beams = beam_weight.shape[1] // 2
    where = jnp.stack([core, lax.axis_index("stn")]).astype(jnp.int32)

    outputs = weights = None
    waiting = []
    before = [chunk for chunk, _ in chunks[1:]]
    arrived = turn(chunks[0][0])
    for number, (_, held) in enumerate(chunks):
        final = number + 1 == len(chunks)
        if weights is None:
            mine, before, spread = lax.optimization_barrier((arrived, before, spread))
            if number == 0:
                spread = spread_middle(spread, inner)
        else:
            mine, before = lax.optimization_barrier((arrived, before))
        if not final:
            arrived = turn(chunks[number + 1][0] if number else before[0])
        other = exchange(mine, "tile", 1)
        if weights is None and (number == 1 or final):
            spread = spread_finish(spread)
            give = lax.dynamic_slice_in_dim(spread, (1 - core) * half_beams, half_beams, 3)
            weights = (spread, exchange(give, "tile", 1))
        for index, slot in enumerate(held):
            fused = weights if final else None
            outputs = correlate(where, mine, other, index, fused, slot, slots, half_beams, outputs)
        if not final:
            waiting.append((mine, other, held))
        if weights is not None:
            if waiting:
                outputs = (outputs[0], form_beams(where, waiting, weights, outputs[1]))
            waiting = []
        outputs = before = lax.optimization_barrier(tuple(outputs))
    return tuple(outputs)


def solution(mesh):
    placed = (P(None, ("band", "stn", "tile"), None), P(), P(None, None, ("band", "stn", "tile")))
    return jax.shard_map(
        per_device,
        mesh=mesh,
        in_specs=placed,
        out_specs=(P(("band", "stn"), None, None, "tile"), P(None, ("band", "stn"), "tile", None)),
        check_vma=False,
    )
```

```python
import functools
import math

import jax
import jax.numpy as jnp
from jax import lax
from jax.experimental import pallas as pl
from jax.experimental.pallas import tpu as pltpu
from jax.sharding import PartitionSpec as P

FINE = 16
TAPS = 4
DUMPS = 2
MD = 256
FRAME_TILE = 128
ROW_TILE = 512
VMEM_LIMIT = 64 * 1024 * 1024


def four_point(values):
    (ar, ai), (br, bi), (cr, ci), (dr, di) = values
    sr, si, tr, ti = ar + cr, ai + ci, ar - cr, ai - ci
    ur, ui, vr, vi = br + dr, bi + di, br - dr, bi - di
    return [(sr + ur, si + ui), (tr + vi, ti - vr), (sr - ur, si - ui), (tr - vi, ti + vr)]


def sixteen_point(values):
    half = math.sqrt(0.5)
    columns = []
    for n2 in range(4):
        column = four_point([values[4 * n1 + n2] for n1 in range(4)])
        for k1 in range(1, 4):
            turn = n2 * k1
            re, im = column[k1]
            if turn == 0:
                continue
            if turn == 2:
                column[k1] = ((re + im) * half, (im - re) * half)
            elif turn == 4:
                column[k1] = (im, -re)
            elif turn == 6:
                column[k1] = ((im - re) * half, -(re + im) * half)
            else:
                co, si = math.cos(math.pi * turn / 8), math.sin(math.pi * turn / 8)
                column[k1] = (re * co + im * si, im * co - re * si)
        columns.append(column)
    result = [None] * 16
    for k1 in range(4):
        row = four_point([columns[n2][k1] for n2 in range(4)])
        for k2 in range(4):
            result[k1 + 4 * k2] = row[k2]
    return result


def channel_body(joined, proto_ref, raw_ref, *refs):
    outs, filtered, held = refs[:-2], refs[-2], refs[-1]
    parts = 1 if joined else len(outs)
    halves = FINE // 8
    lane_shape = (8, raw_ref.shape[2])
    place = lax.broadcasted_iota(jnp.int32, lane_shape, 0)

    def column(start):
        values = jnp.full(lane_shape, proto_ref[start])
        for row in range(1, 8):
            values = jnp.where(place == row, proto_ref[start + row], values)
        return values

    taps = [[column(tap * FINE + half * 8) for half in range(halves)] for tap in range(TAPS)]

    @pl.loop(0, FRAME_TILE // 8)
    def _(step):
        base = pl.multiple_of(step * 8 * FINE, 8 * FINE)
        for part in range(2):
            for half in range(halves):
                rows = [raw_ref[part, pl.ds(base + frame * FINE + half * 8, 8), :] for frame in range(8 + TAPS - 1)]
                for frame in range(8):
                    terms = [rows[frame + tap] * taps[tap][half] for tap in range(TAPS)]
                    total = functools.reduce(lambda left, right: left + right, terms)
                    filtered[part, pl.ds(base + frame * FINE + half * 8, 8), :] = total

    @pl.loop(0, FRAME_TILE // 8)
    def _(step):
        base = pl.multiple_of(step * 8 * FINE, 8 * FINE)
        rows = pl.ds(pl.multiple_of(step * 8, 8), 8)
        values = [
            tuple(filtered[part, pl.ds(base + phase, 8, stride=FINE), :] for part in range(2))
            for phase in range(FINE)
        ]
        for channel, (re, im) in enumerate(sixteen_point(values)):
            held[0, channel, rows, :] = re
            held[1, channel, rows, :] = im

    for channel in range(FINE):
        for part in range(2):
            spectrum = held[part, channel].T.astype(jnp.bfloat16)
            if joined:
                each = outs[0].shape[1]
                outs[0][channel // each, channel % each, part] = spectrum
            else:
                outs[channel % parts][channel // parts, 0, part] = spectrum


def channelize(raw_turned, prototype, dump, per_station, joined):
    inputs_here = raw_turned.shape[2]
    tiles = MD // FRAME_TILE
    span = FRAME_TILE * FINE
    block = span + (TAPS - 1) * FINE
    each = per_station if joined else 1
    count = 1 if joined else per_station
    shape = (FINE // per_station, each, 2, inputs_here, MD)
    return pl.pallas_call(
        functools.partial(channel_body, joined),
        grid=(tiles,),
        in_specs=[
            pl.BlockSpec(memory_space=pltpu.SMEM),
            pl.BlockSpec(
                (pl.Element(2), pl.Element(block), pl.Element(inputs_here)),
                lambda i: (0, (dump * tiles + i) * span, 0),
            ),
        ],
        out_specs=[pl.BlockSpec(shape[:4] + (FRAME_TILE,), lambda i: (0, 0, 0, 0, i))] * count,
        scratch_shapes=[
            pltpu.VMEM((2, span, inputs_here), jnp.float32),
            pltpu.VMEM((2, FINE, FRAME_TILE, inputs_here), jnp.float32),
        ],
        out_shape=[jax.ShapeDtypeStruct(shape, jnp.bfloat16)] * count,
        compiler_params=pltpu.CompilerParams(vmem_limit_bytes=VMEM_LIMIT),
        cost_estimate=pl.CostEstimate(
            flops=MD * inputs_here * FINE * (40 if dump == 0 else 400000),
            bytes_accessed=MD * inputs_here * FINE * 12,
            transcendentals=0,
        ),
        name="channelize",
    )(prototype, raw_turned)


def add_beams(sums, rows, order, weight_ref):
    beams, size = weight_ref.shape[3:]
    weights = [jnp.concatenate([weight_ref[high, low, 0], weight_ref[high, low, 1]], axis=0) for high, low in order]
    if size % 128 == 0:
        weights = [jnp.concatenate(weights, axis=1)]
    wide = rows.shape[0] // len(weights)
    for block, weight in enumerate(weights):
        product = jnp.dot(weight, rows[block * wide:(block + 1) * wide], preferred_element_type=jnp.float32)
        sums[0] += product[:beams, :MD] - product[beams:, MD:]
        sums[1] += product[beams:, :MD] + product[:beams, MD:]


def beams_body(counts, where_ref, mine_weight_ref, other_weight_ref, *refs):
    beam_ref, sums = refs[-2:]
    step = pl.program_id(0)
    inner = mine_weight_ref.shape[1]
    sums[...] = jnp.zeros_like(sums)

    def work(mine_ref, other_ref):
        blocks = mine_ref.shape[0]
        order = [((block ^ where_ref[1]) // inner, (block ^ where_ref[1]) % inner) for block in range(blocks)]
        for rows_ref, weight_ref in ((mine_ref, mine_weight_ref), (other_ref, other_weight_ref)):
            parts = [jnp.concatenate([rows_ref[block, part] for block in range(blocks)], axis=0) for part in range(2)]
            add_beams(sums, jnp.concatenate(parts, axis=1), order, weight_ref)

    start = 0
    for group, count in enumerate(counts):
        @pl.when((step >= start) & (step < start + count))
        def _(group=group):
            work(refs[2 * group], refs[2 * group + 1])

        start += count
    beam_ref[:, 0] = sums[...]


def form_beams(where, groups, weights, earlier):
    blocks, _, _, size, _ = groups[0][0].shape
    outer, inner, _, beams, _ = weights[1].shape
    counts = [len(held) for _, _, held in groups]
    held = [slot for _, _, slots in groups for slot in slots]
    weight_block = (outer, inner, 2, beams, size)
    in_specs = [
        pl.BlockSpec(weight_block, lambda i, where: (0, 0, 0, where[0], 0)),
        pl.BlockSpec(weight_block, lambda i, where: (0, 0, 0, 0, 0)),
    ]
    operands = [where, *weights]
    for group, (mine, other, _) in enumerate(groups):
        start, count = sum(counts[:group]), counts[group]

        def picked(i, where, start=start, count=count):
            return (0, jnp.clip(i - start, 0, count - 1), 0, 0, 0)

        in_specs += [pl.BlockSpec((blocks, None, 2, size, MD), picked)] * 2
        operands += [mine, other]

    def target(i, where):
        return (0, sum(jnp.where(i == step, slot, 0) for step, slot in enumerate(held)), 0, 0)

    return pl.pallas_call(
        functools.partial(beams_body, counts),
        grid_spec=pltpu.PrefetchScalarGridSpec(
            num_scalar_prefetch=1,
            grid=(len(held),),
            in_specs=in_specs + [pl.BlockSpec(memory_space=pl.ANY)],
            out_specs=pl.BlockSpec((2, 1, beams, MD), target),
            scratch_shapes=[pltpu.VMEM((2, beams, MD), jnp.float32)],
        ),
        out_shape=jax.ShapeDtypeStruct(earlier.shape, earlier.dtype),
        input_output_aliases={len(operands): 0},
        compiler_params=pltpu.CompilerParams(vmem_limit_bytes=VMEM_LIMIT),
        cost_estimate=pl.CostEstimate(
            flops=len(held) * 16 * MD * blocks * size * beams,
            bytes_accessed=len(held) * 8 * MD * blocks * size,
            transcendentals=0,
        ),
        name="form_beams",
    )(*operands, earlier)


def correlate_body(with_beams, where_ref, cols_ref, other_ref, *refs):
    mine_weight_ref, other_weight_ref = refs[:2] if with_beams else (None, None)
    vis_ref, straight, twisted = refs[-5], refs[-2], refs[-1]
    beam_ref, sums = refs[-4], refs[-3]
    place = where_ref[1]
    step = pl.program_id(0)
    steps = pl.num_programs(0) // 2
    blocks, _, size, _ = cols_ref.shape
    here = other_ref.shape[0]
    tall = here * size

    @pl.when(step == 0)
    def _():
        for block in range(blocks):
            span = pl.ds(block * size, size)
            re, im = cols_ref[block, 0], cols_ref[block, 1]
            straight[span, :MD] = re
            straight[span, MD:] = im
            twisted[span, :MD] = -im
            twisted[span, MD:] = re
        if with_beams:
            sums[...] = jnp.zeros_like(sums)

    def work(left, weight_ref):
        contract = (((1,), (1,)), ((), ()))
        for part, right in ((0, straight), (1, twisted)):
            product = lax.dot_general(left, right[...], contract, preferred_element_type=jnp.float32)
            vis_ref[0, part] = (product * (1.0 / MD)).astype(jnp.bfloat16)
        if with_beams:
            inner = weight_ref.shape[1]
            add_beams(sums, left, [((block // inner) ^ ((place // inner) % (here // inner)), (block ^ place) % inner) for block in range(here)], weight_ref)

    @pl.when(step < steps)
    def _():
        work(straight[pl.ds(pl.multiple_of(step * tall, tall), tall), :], mine_weight_ref)

    @pl.when(step >= steps)
    def _():
        parts = [jnp.concatenate([other_ref[block, part] for block in range(here)], axis=0) for part in range(2)]
        work(jnp.concatenate(parts, axis=1), other_weight_ref)

    if with_beams:
        @pl.when(step == 2 * steps - 1)
        def _():
            beam_ref[:, 0] = sums[...]


def correlate(where, mine, other, index, weights, slot, slots, beams, earlier):
    blocks, _, _, size, _ = mine.shape
    width = blocks * size
    here = min(blocks, ROW_TILE // size)
    steps = blocks // here
    beam_shape = (2, slots, beams, MD)

    def clipped(step, half):
        return jnp.maximum(step - steps, 0) if half else jnp.minimum(step, steps - 1)

    in_specs = [
        pl.BlockSpec((blocks, None, 2, size, MD), lambda i, where: (0, index, 0, 0, 0)),
        pl.BlockSpec((here, None, 2, size, MD), lambda i, where: (clipped(i, 1), index, 0, 0, 0)),
    ]
    operands = [where, mine, other]
    if weights is not None:
        inner = weights[0].shape[1]
        weight_block = (here // inner, inner, 2, beams, size)
        in_specs += [
            pl.BlockSpec(weight_block, lambda i, where: (clipped(i, 0) ^ (where[1] // here), 0, 0, where[0], 0)),
            pl.BlockSpec(weight_block, lambda i, where: (clipped(i, 1) ^ (where[1] // here), 0, 0, 0, 0)),
        ]
        operands += list(weights)
        beam_spec = pl.BlockSpec((2, 1, beams, MD), lambda i, where: (0, slot, 0, 0))
    else:
        beam_spec = pl.BlockSpec(memory_space=pl.ANY)
    aliases = {}
    if earlier is not None:
        aliases = {len(operands): 0, len(operands) + 1: 1}
        in_specs += [pl.BlockSpec(memory_space=pl.ANY)] * 2
        operands += list(earlier)
    return pl.pallas_call(
        functools.partial(correlate_body, weights is not None),
        grid_spec=pltpu.PrefetchScalarGridSpec(
            num_scalar_prefetch=1,
            grid=(2 * steps,),
            in_specs=in_specs,
            out_specs=[
                pl.BlockSpec(
                    (1, 2, here * size, width),
                    lambda i, where: (slot, 0, (where[0] ^ (i // steps)) * steps + i % steps, 0),
                ),
                beam_spec,
            ],
            scratch_shapes=[
                pltpu.VMEM((2, beams, MD) if weights is not None else (8, 128), jnp.float32),
                pltpu.VMEM((width, 2 * MD), jnp.bfloat16),
                pltpu.VMEM((width, 2 * MD), jnp.bfloat16),
            ],
        ),
        out_shape=[
            jax.ShapeDtypeStruct((slots, 2, 2 * width, width), jnp.bfloat16),
            jax.ShapeDtypeStruct(beam_shape, jnp.float32),
        ],
        input_output_aliases=aliases,
        compiler_params=pltpu.CompilerParams(vmem_limit_bytes=VMEM_LIMIT),
        cost_estimate=pl.CostEstimate(
            flops=16 * MD * width * width, bytes_accessed=10 * width * width, transcendentals=0
        ),
        name="correlate",
    )(*operands)


def exchange(values, axis, turn):
    count = lax.axis_size(axis)
    return lax.ppermute(values, axis, [(index, index ^ turn) for index in range(count)])


def spread_start(weight, ready, inner):
    stations = lax.axis_size("stn")
    outer = stations // inner
    if outer != 4:
        place = lax.axis_index("stn")
        gathered = jnp.take(lax.all_gather(weight, "stn"), place ^ jnp.arange(stations), axis=0)
        return gathered.reshape((outer, inner) + weight.shape), ready
    opposite, ready = lax.optimization_barrier((exchange(weight, "stn", 2 * inner), ready))
    pair = jnp.stack([weight, opposite])
    return (pair, exchange(pair, "stn", 1), exchange(pair, "stn", inner)), ready


def spread_middle(held, inner):
    if not isinstance(held, tuple):
        return held
    return held + (exchange(held[2], "stn", 1),)


def spread_finish(held):
    if not isinstance(held, tuple):
        return held
    pair, beside, side, across = held
    return jnp.stack(
        [
            jnp.stack([pair[0], beside[0]]),
            jnp.stack([side[0], across[0]]),
            jnp.stack([pair[1], beside[1]]),
            jnp.stack([side[1], across[1]]),
        ]
    )


def per_device(raw_samples, prototype, beam_weight):
    stations = lax.axis_size("stn")
    core = lax.axis_index("tile")
    inner = 2
    slots = FINE * DUMPS // stations
    per_dump = max(1, slots // DUMPS)
    turn = functools.partial(lax.all_to_all, axis_name="stn", split_axis=0, concat_axis=0, tiled=True)

    raw_turned = raw_samples.transpose(0, 2, 1)
    spectra = [channelize(raw_turned, prototype, 0, per_dump, True)]
    spread, raw_turned = spread_start(beam_weight, raw_turned, inner)
    spectra += [channelize(raw_turned, prototype, dump, per_dump, False) for dump in range(1, DUMPS)]
    if slots >= DUMPS:
        chunks = [(part, [DUMPS * index for index in range(per_dump)]) for part in spectra[0]]
        chunks += [(part, [DUMPS * index + 1]) for index, part in enumerate(spectra[1])]
    else:
        whole = jnp.stack([spectra[dump][0] for dump in range(DUMPS)], axis=1)
        chunks = [(whole.reshape((stations,) + whole.shape[2:]), [0])]

    half_beams = beam_weight.shape[1] // 2
    where = jnp.stack([core, lax.axis_index("stn")]).astype(jnp.int32)

    outputs = weights = None
    waiting = []
    before = [chunk for chunk, _ in chunks[1:]]
    arrived = turn(chunks[0][0])
    for number, (_, held) in enumerate(chunks):
        final = number + 1 == len(chunks)
        if weights is None:
            mine, before, spread = lax.optimization_barrier((arrived, before, spread))
            if number == 0:
                spread = spread_middle(spread, inner)
        else:
            mine, before = lax.optimization_barrier((arrived, before))
        if not final:
            arrived = turn(chunks[number + 1][0] if number else before[0])
        other = exchange(mine, "tile", 1)
        if weights is None and (number == 1 or final):
            spread = spread_finish(spread)
            give = lax.dynamic_slice_in_dim(spread, (1 - core) * half_beams, half_beams, 3)
            weights = (spread, exchange(give, "tile", 1))
        for index, slot in enumerate(held):
            fused = weights if final else None
            outputs = correlate(where, mine, other, index, fused, slot, slots, half_beams, outputs)
        if not final:
            waiting.append((mine, other, held))
        if weights is not None:
            if waiting:
                outputs = (outputs[0], form_beams(where, waiting, weights, outputs[1]))
            waiting = []
        outputs = before = lax.optimization_barrier(tuple(outputs))
    return tuple(outputs)


def solution(mesh):
    placed = (P(None, ("band", "stn", "tile"), None), P(), P(None, None, ("band", "stn", "tile")))
    return jax.shard_map(
        per_device,
        mesh=mesh,
        in_specs=placed,
        out_specs=(P(("band", "stn"), None, None, "tile"), P(None, ("band", "stn"), "tile", None)),
        check_vma=False,
    )
```

```python
import functools
import math

import jax
import jax.numpy as jnp
from jax import lax
from jax.experimental import pallas as pl
from jax.experimental.pallas import tpu as pltpu
from jax.sharding import PartitionSpec as P

FINE = 16
TAPS = 4
DUMPS = 2
MD = 256
FRAME_TILE = 128
STAGES = 3
VMEM_LIMIT = 64 * 1024 * 1024


def four_point(values):
    (ar, ai), (br, bi), (cr, ci), (dr, di) = values
    sr, si, tr, ti = ar + cr, ai + ci, ar - cr, ai - ci
    ur, ui, vr, vi = br + dr, bi + di, br - dr, bi - di
    return [(sr + ur, si + ui), (tr + vi, ti - vr), (sr - ur, si - ui), (tr - vi, ti + vr)]


def sixteen_point(values):
    half = math.sqrt(0.5)
    columns = []
    for n2 in range(4):
        column = four_point([values[4 * n1 + n2] for n1 in range(4)])
        for k1 in range(1, 4):
            turn = n2 * k1
            re, im = column[k1]
            if turn == 0:
                continue
            if turn == 2:
                column[k1] = ((re + im) * half, (im - re) * half)
            elif turn == 4:
                column[k1] = (im, -re)
            elif turn == 6:
                column[k1] = ((im - re) * half, -(re + im) * half)
            else:
                co, si = math.cos(math.pi * turn / 8), math.sin(math.pi * turn / 8)
                column[k1] = (re * co + im * si, im * co - re * si)
        columns.append(column)
    result = [None] * 16
    for k1 in range(4):
        row = four_point([columns[n2][k1] for n2 in range(4)])
        for k2 in range(4):
            result[k1 + 4 * k2] = row[k2]
    return result


def channel_body(joined, proto_ref, raw_ref, *refs):
    outs, filtered, held = refs[:-2], refs[-2], refs[-1]
    parts = 1 if joined else len(outs)
    halves = FINE // 8
    lane_shape = (8, raw_ref.shape[2])
    place = lax.broadcasted_iota(jnp.int32, lane_shape, 0)

    def column(start):
        values = jnp.full(lane_shape, proto_ref[start])
        for row in range(1, 8):
            values = jnp.where(place == row, proto_ref[start + row], values)
        return values

    taps = [[column(tap * FINE + half * 8) for half in range(halves)] for tap in range(TAPS)]

    @pl.loop(0, FRAME_TILE // 8)
    def _(step):
        base = pl.multiple_of(step * 8 * FINE, 8 * FINE)
        for part in range(2):
            for half in range(halves):
                rows = [raw_ref[part, pl.ds(base + frame * FINE + half * 8, 8), :] for frame in range(8 + TAPS - 1)]
                for frame in range(8):
                    terms = [rows[frame + tap] * taps[tap][half] for tap in range(TAPS)]
                    total = functools.reduce(lambda left, right: left + right, terms)
                    filtered[part, pl.ds(base + frame * FINE + half * 8, 8), :] = total

    @pl.loop(0, FRAME_TILE // 8)
    def _(step):
        base = pl.multiple_of(step * 8 * FINE, 8 * FINE)
        rows = pl.ds(pl.multiple_of(step * 8, 8), 8)
        values = [
            tuple(filtered[part, pl.ds(base + phase, 8, stride=FINE), :] for part in range(2))
            for phase in range(FINE)
        ]
        for channel, (re, im) in enumerate(sixteen_point(values)):
            held[0, channel, rows, :] = re
            held[1, channel, rows, :] = im

    for channel in range(FINE):
        for part in range(2):
            spectrum = held[part, channel].T.astype(jnp.bfloat16)
            if joined:
                each = outs[0].shape[1]
                outs[0][channel // each, channel % each, part] = spectrum
            else:
                outs[channel % parts][channel // parts, 0, part] = spectrum


def channelize(raw_turned, prototype, dump, per_station, joined):
    inputs_here = raw_turned.shape[2]
    tiles = MD // FRAME_TILE
    span = FRAME_TILE * FINE
    block = span + (TAPS - 1) * FINE
    each = per_station if joined else 1
    count = 1 if joined else per_station
    shape = (FINE // per_station, each, 2, inputs_here, MD)
    return pl.pallas_call(
        functools.partial(channel_body, joined),
        grid=(tiles,),
        in_specs=[
            pl.BlockSpec(memory_space=pltpu.SMEM),
            pl.BlockSpec(
                (pl.Element(2), pl.Element(block), pl.Element(inputs_here)),
                lambda i: (0, (dump * tiles + i) * span, 0),
            ),
        ],
        out_specs=[pl.BlockSpec(shape[:4] + (FRAME_TILE,), lambda i: (0, 0, 0, 0, i))] * count,
        scratch_shapes=[
            pltpu.VMEM((2, span, inputs_here), jnp.float32),
            pltpu.VMEM((2, FINE, FRAME_TILE, inputs_here), jnp.float32),
        ],
        out_shape=[jax.ShapeDtypeStruct(shape, jnp.bfloat16)] * count,
        compiler_params=pltpu.CompilerParams(vmem_limit_bytes=VMEM_LIMIT),
        cost_estimate=pl.CostEstimate(
            flops=MD * inputs_here * FINE * (40 if dump == 0 else 400000),
            bytes_accessed=MD * inputs_here * FINE * 12,
            transcendentals=0,
        ),
        name="channelize",
    )(prototype, raw_turned)


def add_beams(sums, rows, order, weight_ref):
    beams, size = weight_ref.shape[3:]
    weights = [jnp.concatenate([weight_ref[high, low, 0], weight_ref[high, low, 1]], axis=0) for high, low in order]
    if size % 128 == 0:
        weights = [jnp.concatenate(weights, axis=1)]
    wide = rows.shape[0] // len(weights)
    for block, weight in enumerate(weights):
        product = jnp.dot(weight, rows[block * wide:(block + 1) * wide], preferred_element_type=jnp.float32)
        sums[0] += product[:beams, :MD] - product[beams:, MD:]
        sums[1] += product[beams:, :MD] + product[:beams, MD:]


def beams_body(counts, where_ref, mine_weight_ref, other_weight_ref, *refs):
    beam_ref, sums = refs[-2:]
    step = pl.program_id(0)
    inner = mine_weight_ref.shape[1]
    sums[...] = jnp.zeros_like(sums)

    def work(mine_ref, other_ref):
        blocks = mine_ref.shape[0]
        order = [((block ^ where_ref[1]) // inner, (block ^ where_ref[1]) % inner) for block in range(blocks)]
        for rows_ref, weight_ref in ((mine_ref, mine_weight_ref), (other_ref, other_weight_ref)):
            parts = [jnp.concatenate([rows_ref[block, part] for block in range(blocks)], axis=0) for part in range(2)]
            add_beams(sums, jnp.concatenate(parts, axis=1), order, weight_ref)

    start = 0
    for group, count in enumerate(counts):
        @pl.when((step >= start) & (step < start + count))
        def _(group=group):
            work(refs[2 * group], refs[2 * group + 1])

        start += count
    beam_ref[:, 0] = sums[...]


def form_beams(where, groups, weights, earlier):
    blocks, _, _, size, _ = groups[0][0].shape
    outer, inner, _, beams, _ = weights[1].shape
    counts = [len(held) for _, _, held in groups]
    held = [slot for _, _, slots in groups for slot in slots]
    weight_block = (outer, inner, 2, beams, size)
    in_specs = [
        pl.BlockSpec(weight_block, lambda i, where: (0, 0, 0, where[0], 0)),
        pl.BlockSpec(weight_block, lambda i, where: (0, 0, 0, 0, 0)),
    ]
    operands = [where, *weights]
    for group, (mine, other, _) in enumerate(groups):
        start, count = sum(counts[:group]), counts[group]

        def picked(i, where, start=start, count=count):
            return (0, jnp.clip(i - start, 0, count - 1), 0, 0, 0)

        in_specs += [pl.BlockSpec((blocks, None, 2, size, MD), picked)] * 2
        operands += [mine, other]

    def target(i, where):
        return (0, sum(jnp.where(i == step, slot, 0) for step, slot in enumerate(held)), 0, 0)

    return pl.pallas_call(
        functools.partial(beams_body, counts),
        grid_spec=pltpu.PrefetchScalarGridSpec(
            num_scalar_prefetch=1,
            grid=(len(held),),
            in_specs=in_specs + [pl.BlockSpec(memory_space=pl.ANY)],
            out_specs=pl.BlockSpec((2, 1, beams, MD), target),
            scratch_shapes=[pltpu.VMEM((2, beams, MD), jnp.float32)],
        ),
        out_shape=jax.ShapeDtypeStruct(earlier.shape, earlier.dtype),
        input_output_aliases={len(operands): 0},
        compiler_params=pltpu.CompilerParams(vmem_limit_bytes=VMEM_LIMIT),
        cost_estimate=pl.CostEstimate(
            flops=len(held) * 16 * MD * blocks * size * beams,
            bytes_accessed=len(held) * 8 * MD * blocks * size,
            transcendentals=0,
        ),
        name="form_beams",
    )(*operands, earlier)


def correlate_body(halves, index, slot, with_beams, where_ref, cols_ref, *refs):
    other_ref = refs[0]
    if with_beams:
        sources = refs[1:3]
        vis_ref, beam_ref, straight, twisted, others, far, stage, load_sems, stage_sems = refs[-12:-3]
        sums, mine_weight, other_weight = refs[-3:]
        beams = mine_weight.shape[3]
    else:
        vis_ref, beam_ref, straight, twisted, others, far, stage, load_sems, stage_sems = refs[-9:]
    core, place = where_ref[0], where_ref[1]
    blocks, _, size, _ = cols_ref.shape
    buffers, width, _ = stage.shape
    loads = []
    if 1 in halves:
        loads.append(pltpu.make_async_copy(other_ref.at[:, index], others, load_sems.at[0]))
    if with_beams:
        mine_half = sources[0].at[:, :, :, pl.ds(pl.multiple_of(core * beams, beams), beams)]
        loads.append(pltpu.make_async_copy(mine_half, mine_weight, load_sems.at[1]))
        loads.append(pltpu.make_async_copy(sources[1], other_weight, load_sems.at[2]))
    for load in loads:
        load.start()
    for block in range(blocks):
        span = slice(block * size, (block + 1) * size)
        re, im = cols_ref[block, 0], cols_ref[block, 1]
        straight[span, :MD] = re
        straight[span, MD:] = im
        twisted[span, :MD] = -im
        twisted[span, MD:] = re

    contract = (((1,), (1,)), ((), ()))
    stores = []

    def correlate_half(half, left):
        start = pl.multiple_of((core ^ half) * width, width)
        for part, right in ((0, straight), (1, twisted)):
            pieces = 2 if part == 1 and half == halves[-1] else 1
            for column in range(pieces):
                piece = width // pieces
                span = slice(column * piece, (column + 1) * piece)
                buffer = len(stores) % buffers
                if len(stores) >= buffers:
                    stores[len(stores) - buffers].wait()
                product = lax.dot_general(left[...], right[span, :], contract, preferred_element_type=jnp.float32)
                stage[buffer, :, :piece] = (product * (1.0 / MD)).astype(jnp.bfloat16)
                source = stage.at[buffer, :, pl.ds(0, piece)]
                target = vis_ref.at[slot, part, pl.ds(start, width), pl.ds(column * piece, piece)]
                stores.append(pltpu.make_async_copy(source, target, stage_sems.at[buffer]))
                stores[-1].start()

    if 0 in halves:
        correlate_half(0, straight)
    if 1 in halves:
        loads[0].wait()
        for block in range(blocks):
            span = slice(block * size, (block + 1) * size)
            far[span, :MD] = others[block, 0]
            far[span, MD:] = others[block, 1]
    if with_beams:
        loads[1].wait()
        loads[2].wait()
        inner = mine_weight.shape[1]
        order = [((block ^ place) // inner, (block ^ place) % inner) for block in range(blocks)]
        sums[...] = jnp.zeros_like(sums)
        @pl.when(core >= 0)
        def _():
            add_beams(sums, straight[...], order, mine_weight)
            add_beams(sums, far[...], order, other_weight)

        beam_store = pltpu.make_async_copy(sums, beam_ref.at[:, slot], load_sems.at[0])
        beam_store.start()
    if 1 in halves:
        correlate_half(1, far)
    for store in stores[-buffers:]:
        store.wait()
    if with_beams:
        beam_store.wait()


def correlate(where, mine, other, halves, index, weights, slot, slots, beams, earlier):
    blocks, _, _, size, _ = mine.shape
    width = blocks * size
    any_spec = pl.BlockSpec(memory_space=pl.ANY)
    in_specs = [pl.BlockSpec((blocks, None, 2, size, MD), lambda i, where: (0, index, 0, 0, 0))]
    operands = [where, mine]
    if 1 in halves:
        in_specs.append(any_spec)
        operands.append(other)
    scratch = [
        pltpu.VMEM((width, 2 * MD), jnp.bfloat16),
        pltpu.VMEM((width, 2 * MD), jnp.bfloat16),
        pltpu.VMEM((blocks, 2, size, MD), jnp.bfloat16),
        pltpu.VMEM((width, 2 * MD), jnp.bfloat16),
        pltpu.VMEM((STAGES, width, width), jnp.bfloat16),
        pltpu.SemaphoreType.DMA((3,)),
        pltpu.SemaphoreType.DMA((STAGES,)),
    ]
    if weights is not None:
        in_specs += [any_spec] * 2
        operands += list(weights)
        scratch.append(pltpu.VMEM((2, beams, MD), jnp.float32))
        scratch += [pltpu.VMEM(weights[1].shape, jnp.bfloat16)] * 2
    aliases = {}
    if earlier is not None:
        aliases = {len(operands): 0, len(operands) + 1: 1}
        in_specs += [any_spec] * 2
        operands += list(earlier)
    return pl.pallas_call(
        functools.partial(correlate_body, halves, index, slot, weights is not None),
        grid_spec=pltpu.PrefetchScalarGridSpec(
            num_scalar_prefetch=1,
            grid=(1,),
            in_specs=in_specs,
            out_specs=[any_spec, any_spec],
            scratch_shapes=scratch,
        ),
        out_shape=[
            jax.ShapeDtypeStruct((slots, 2, 2 * width, width), jnp.bfloat16),
            jax.ShapeDtypeStruct((2, slots, beams, MD), jnp.float32),
        ],
        input_output_aliases=aliases,
        compiler_params=pltpu.CompilerParams(vmem_limit_bytes=VMEM_LIMIT),
        cost_estimate=pl.CostEstimate(
            flops=8 * len(halves) * MD * width * width, bytes_accessed=5 * len(halves) * width * width, transcendentals=0
        ),
        name="correlate",
    )(*operands)


def exchange(values, axis, turn):
    count = lax.axis_size(axis)
    return lax.ppermute(values, axis, [(index, index ^ turn) for index in range(count)])


def spread_start(weight, ready, inner):
    stations = lax.axis_size("stn")
    outer = stations // inner
    if outer != 4:
        place = lax.axis_index("stn")
        gathered = jnp.take(lax.all_gather(weight, "stn"), place ^ jnp.arange(stations), axis=0)
        return gathered.reshape((outer, inner) + weight.shape), ready
    opposite, ready = lax.optimization_barrier((exchange(weight, "stn", 2 * inner), ready))
    pair = jnp.stack([weight, opposite])
    return (pair, exchange(pair, "stn", 1), exchange(pair, "stn", inner)), ready


def spread_middle(held, inner):
    if not isinstance(held, tuple):
        return held
    return held + (exchange(held[2], "stn", 1),)


def spread_finish(held):
    if not isinstance(held, tuple):
        return held
    pair, beside, side, across = held
    return jnp.stack(
        [
            jnp.stack([pair[0], beside[0]]),
            jnp.stack([side[0], across[0]]),
            jnp.stack([pair[1], beside[1]]),
            jnp.stack([side[1], across[1]]),
        ]
    )


def per_device(raw_samples, prototype, beam_weight):
    stations = lax.axis_size("stn")
    core = lax.axis_index("tile")
    inner = 2
    slots = FINE * DUMPS // stations
    per_dump = max(1, slots // DUMPS)
    turn = functools.partial(lax.all_to_all, axis_name="stn", split_axis=0, concat_axis=0, tiled=True)

    raw_turned = raw_samples.transpose(0, 2, 1)
    spectra = [channelize(raw_turned, prototype, 0, per_dump, True)]
    spread, raw_turned = spread_start(beam_weight, raw_turned, inner)
    spectra += [channelize(raw_turned, prototype, dump, per_dump, False) for dump in range(1, DUMPS)]
    if slots >= DUMPS:
        chunks = [(part, [DUMPS * index for index in range(per_dump)]) for part in spectra[0]]
        chunks += [(part, [DUMPS * index + 1]) for index, part in enumerate(spectra[1])]
    else:
        whole = jnp.stack([spectra[dump][0] for dump in range(DUMPS)], axis=1)
        chunks = [(whole.reshape((stations,) + whole.shape[2:]), [0])]

    half_beams = beam_weight.shape[1] // 2
    where = jnp.stack([core, lax.axis_index("stn")]).astype(jnp.int32)

    outputs = weights = None
    waiting = []
    before = [chunk for chunk, _ in chunks[1:]]
    arrived = turn(chunks[0][0])
    for number, (_, held) in enumerate(chunks):
        final = number + 1 == len(chunks)
        if weights is None:
            mine, before, spread = lax.optimization_barrier((arrived, before, spread))
            if number == 0:
                spread = spread_middle(spread, inner)
        else:
            mine, before = lax.optimization_barrier((arrived, before))
        if not final:
            arrived = turn(chunks[number + 1][0] if number else before[0])
        other = exchange(mine, "tile", 1)
        if weights is None and (number == 1 or final):
            spread = spread_finish(spread)
            give = lax.dynamic_slice_in_dim(spread, (1 - core) * half_beams, half_beams, 3)
            weights = (spread, exchange(give, "tile", 1))
        for index, slot in enumerate(held):
            fused = weights if final else None
            outputs = correlate(where, mine, other, (0, 1), index, fused, slot, slots, half_beams, outputs)
        if not final:
            waiting.append((mine, other, held))
        if weights is not None:
            if waiting:
                outputs = (outputs[0], form_beams(where, waiting, weights, outputs[1]))
            waiting = []
        outputs = before = lax.optimization_barrier(tuple(outputs))
    return tuple(outputs)


def solution(mesh):
    placed = (P(None, ("band", "stn", "tile"), None), P(), P(None, None, ("band", "stn", "tile")))
    return jax.shard_map(
        per_device,
        mesh=mesh,
        in_specs=placed,
        out_specs=(P(("band", "stn"), None, None, "tile"), P(None, ("band", "stn"), "tile", None)),
        check_vma=False,
    )
```

```python
import functools
import math

import jax
import jax.numpy as jnp
from jax import lax
from jax.experimental import pallas as pl
from jax.experimental.pallas import tpu as pltpu
from jax.sharding import PartitionSpec as P

FINE = 16
TAPS = 4
DUMPS = 2
MD = 256
FRAME_TILE = 128
STAGES = 3
VMEM_LIMIT = 64 * 1024 * 1024


def four_point(values):
    (ar, ai), (br, bi), (cr, ci), (dr, di) = values
    sr, si, tr, ti = ar + cr, ai + ci, ar - cr, ai - ci
    ur, ui, vr, vi = br + dr, bi + di, br - dr, bi - di
    return [(sr + ur, si + ui), (tr + vi, ti - vr), (sr - ur, si - ui), (tr - vi, ti + vr)]


def sixteen_point(values):
    half = math.sqrt(0.5)
    columns = []
    for n2 in range(4):
        column = four_point([values[4 * n1 + n2] for n1 in range(4)])
        for k1 in range(1, 4):
            turn = n2 * k1
            re, im = column[k1]
            if turn == 0:
                continue
            if turn == 2:
                column[k1] = ((re + im) * half, (im - re) * half)
            elif turn == 4:
                column[k1] = (im, -re)
            elif turn == 6:
                column[k1] = ((im - re) * half, -(re + im) * half)
            else:
                co, si = math.cos(math.pi * turn / 8), math.sin(math.pi * turn / 8)
                column[k1] = (re * co + im * si, im * co - re * si)
        columns.append(column)
    result = [None] * 16
    for k1 in range(4):
        row = four_point([columns[n2][k1] for n2 in range(4)])
        for k2 in range(4):
            result[k1 + 4 * k2] = row[k2]
    return result


def channel_body(joined, proto_ref, raw_ref, *refs):
    outs, filtered, held = refs[:-2], refs[-2], refs[-1]
    parts = 1 if joined else len(outs)
    halves = FINE // 8
    lane_shape = (8, raw_ref.shape[2])
    place = lax.broadcasted_iota(jnp.int32, lane_shape, 0)

    def column(start):
        values = jnp.full(lane_shape, proto_ref[start])
        for row in range(1, 8):
            values = jnp.where(place == row, proto_ref[start + row], values)
        return values

    taps = [[column(tap * FINE + half * 8) for half in range(halves)] for tap in range(TAPS)]

    @pl.loop(0, FRAME_TILE // 8)
    def _(step):
        base = pl.multiple_of(step * 8 * FINE, 8 * FINE)
        for part in range(2):
            for half in range(halves):
                rows = [raw_ref[part, pl.ds(base + frame * FINE + half * 8, 8), :] for frame in range(8 + TAPS - 1)]
                for frame in range(8):
                    terms = [rows[frame + tap] * taps[tap][half] for tap in range(TAPS)]
                    total = functools.reduce(lambda left, right: left + right, terms)
                    filtered[part, pl.ds(base + frame * FINE + half * 8, 8), :] = total

    @pl.loop(0, FRAME_TILE // 8)
    def _(step):
        base = pl.multiple_of(step * 8 * FINE, 8 * FINE)
        rows = pl.ds(pl.multiple_of(step * 8, 8), 8)
        values = [
            tuple(filtered[part, pl.ds(base + phase, 8, stride=FINE), :] for part in range(2))
            for phase in range(FINE)
        ]
        for channel, (re, im) in enumerate(sixteen_point(values)):
            held[0, channel, rows, :] = re
            held[1, channel, rows, :] = im

    for channel in range(FINE):
        for part in range(2):
            spectrum = held[part, channel].T.astype(jnp.bfloat16)
            if joined:
                each = outs[0].shape[1]
                outs[0][channel // each, channel % each, part] = spectrum
            else:
                outs[channel % parts][channel // parts, 0, part] = spectrum


def channelize(raw_turned, prototype, dump, per_station, joined):
    inputs_here = raw_turned.shape[2]
    tiles = MD // FRAME_TILE
    span = FRAME_TILE * FINE
    block = span + (TAPS - 1) * FINE
    each = per_station if joined else 1
    count = 1 if joined else per_station
    shape = (FINE // per_station, each, 2, inputs_here, MD)
    return pl.pallas_call(
        functools.partial(channel_body, joined),
        grid=(tiles,),
        in_specs=[
            pl.BlockSpec(memory_space=pltpu.SMEM),
            pl.BlockSpec(
                (pl.Element(2), pl.Element(block), pl.Element(inputs_here)),
                lambda i: (0, (dump * tiles + i) * span, 0),
            ),
        ],
        out_specs=[pl.BlockSpec(shape[:4] + (FRAME_TILE,), lambda i: (0, 0, 0, 0, i))] * count,
        scratch_shapes=[
            pltpu.VMEM((2, span, inputs_here), jnp.float32),
            pltpu.VMEM((2, FINE, FRAME_TILE, inputs_here), jnp.float32),
        ],
        out_shape=[jax.ShapeDtypeStruct(shape, jnp.bfloat16)] * count,
        compiler_params=pltpu.CompilerParams(vmem_limit_bytes=VMEM_LIMIT),
        cost_estimate=pl.CostEstimate(
            flops=MD * inputs_here * FINE * (40 if dump == 0 else 400000),
            bytes_accessed=MD * inputs_here * FINE * 12,
            transcendentals=0,
        ),
        name="channelize",
    )(prototype, raw_turned)


def add_beams(sums, rows, order, weight_ref):
    beams, size = weight_ref.shape[3:]
    weights = [jnp.concatenate([weight_ref[high, low, 0], weight_ref[high, low, 1]], axis=0) for high, low in order]
    if size % 128 == 0:
        weights = [jnp.concatenate(weights, axis=1)]
    wide = rows.shape[0] // len(weights)
    for block, weight in enumerate(weights):
        product = jnp.dot(weight, rows[block * wide:(block + 1) * wide], preferred_element_type=jnp.float32)
        sums[0] += product[:beams, :MD] - product[beams:, MD:]
        sums[1] += product[beams:, :MD] + product[:beams, MD:]


def beams_body(counts, where_ref, mine_weight_ref, other_weight_ref, *refs):
    beam_ref, sums = refs[-2:]
    step = pl.program_id(0)
    inner = mine_weight_ref.shape[1]
    sums[...] = jnp.zeros_like(sums)

    def work(mine_ref, other_ref):
        blocks = mine_ref.shape[0]
        order = [((block ^ where_ref[1]) // inner, (block ^ where_ref[1]) % inner) for block in range(blocks)]
        for rows_ref, weight_ref in ((mine_ref, mine_weight_ref), (other_ref, other_weight_ref)):
            parts = [jnp.concatenate([rows_ref[block, part] for block in range(blocks)], axis=0) for part in range(2)]
            add_beams(sums, jnp.concatenate(parts, axis=1), order, weight_ref)

    start = 0
    for group, count in enumerate(counts):
        @pl.when((step >= start) & (step < start + count))
        def _(group=group):
            work(refs[2 * group], refs[2 * group + 1])

        start += count
    beam_ref[:, 0] = sums[...]


def form_beams(where, groups, weights, earlier):
    blocks, _, _, size, _ = groups[0][0].shape
    outer, inner, _, beams, _ = weights[1].shape
    counts = [len(held) for _, _, held in groups]
    held = [slot for _, _, slots in groups for slot in slots]
    weight_block = (outer, inner, 2, beams, size)
    in_specs = [
        pl.BlockSpec(weight_block, lambda i, where: (0, 0, 0, where[0], 0)),
        pl.BlockSpec(weight_block, lambda i, where: (0, 0, 0, 0, 0)),
    ]
    operands = [where, *weights]
    for group, (mine, other, _) in enumerate(groups):
        start, count = sum(counts[:group]), counts[group]

        def picked(i, where, start=start, count=count):
            return (0, jnp.clip(i - start, 0, count - 1), 0, 0, 0)

        in_specs += [pl.BlockSpec((blocks, None, 2, size, MD), picked)] * 2
        operands += [mine, other]

    def target(i, where):
        return (0, sum(jnp.where(i == step, slot, 0) for step, slot in enumerate(held)), 0, 0)

    return pl.pallas_call(
        functools.partial(beams_body, counts),
        grid_spec=pltpu.PrefetchScalarGridSpec(
            num_scalar_prefetch=1,
            grid=(len(held),),
            in_specs=in_specs + [pl.BlockSpec(memory_space=pl.ANY)],
            out_specs=pl.BlockSpec((2, 1, beams, MD), target),
            scratch_shapes=[pltpu.VMEM((2, beams, MD), jnp.float32)],
        ),
        out_shape=jax.ShapeDtypeStruct(earlier.shape, earlier.dtype),
        input_output_aliases={len(operands): 0},
        compiler_params=pltpu.CompilerParams(vmem_limit_bytes=VMEM_LIMIT),
        cost_estimate=pl.CostEstimate(
            flops=len(held) * 16 * MD * blocks * size * beams,
            bytes_accessed=len(held) * 8 * MD * blocks * size,
            transcendentals=0,
        ),
        name="form_beams",
    )(*operands, earlier)


def correlate_body(halves, index, slot, with_beams, where_ref, cols_ref, *refs):
    other_ref = refs[0]
    if with_beams:
        sources = refs[1:3]
        vis_ref, beam_ref, straight, twisted, others, far, stage, load_sems, stage_sems = refs[-12:-3]
        sums, mine_weight, other_weight = refs[-3:]
        beams = mine_weight.shape[3]
    else:
        vis_ref, beam_ref, straight, twisted, others, far, stage, load_sems, stage_sems = refs[-9:]
    core, place = where_ref[0], where_ref[1]
    blocks, _, size, _ = cols_ref.shape
    buffers, width, _ = stage.shape
    loads = []
    if 1 in halves:
        loads.append(pltpu.make_async_copy(other_ref.at[:, index], others, load_sems.at[0]))
    if with_beams:
        mine_half = sources[0].at[:, :, :, pl.ds(pl.multiple_of(core * beams, beams), beams)]
        loads.append(pltpu.make_async_copy(mine_half, mine_weight, load_sems.at[1]))
        loads.append(pltpu.make_async_copy(sources[1], other_weight, load_sems.at[2]))
    for load in loads:
        load.start()
    for block in range(blocks):
        span = slice(block * size, (block + 1) * size)
        re, im = cols_ref[block, 0], cols_ref[block, 1]
        straight[span, :MD] = re
        straight[span, MD:] = im

    contract = (((1,), (1,)), ((), ()))
    stores = []

    def turn_columns():
        for block in range(blocks):
            span = slice(block * size, (block + 1) * size)
            twisted[span, :MD] = -cols_ref[block, 1]
            twisted[span, MD:] = cols_ref[block, 0]

    def correlate_half(half, left):
        start = pl.multiple_of((core ^ half) * width, width)
        for part, right in ((0, straight), (1, twisted)):
            pieces = 2 if part == 1 and half == halves[-1] else 1
            if part == 1 and half == halves[0]:
                turn_columns()
            for column in range(pieces):
                piece = width // pieces
                span = slice(column * piece, (column + 1) * piece)
                buffer = len(stores) % buffers
                if len(stores) >= buffers:
                    stores[len(stores) - buffers].wait()
                product = lax.dot_general(left[...], right[span, :], contract, preferred_element_type=jnp.float32)
                stage[buffer, :, :piece] = (product * (1.0 / MD)).astype(jnp.bfloat16)
                source = stage.at[buffer, :, pl.ds(0, piece)]
                target = vis_ref.at[slot, part, pl.ds(start, width), pl.ds(column * piece, piece)]
                stores.append(pltpu.make_async_copy(source, target, stage_sems.at[buffer]))
                stores[-1].start()

    if 0 in halves:
        correlate_half(0, straight)
    if 1 in halves:
        loads[0].wait()
        for block in range(blocks):
            span = slice(block * size, (block + 1) * size)
            far[span, :MD] = others[block, 0]
            far[span, MD:] = others[block, 1]
    if with_beams:
        loads[1].wait()
        loads[2].wait()
        inner = mine_weight.shape[1]
        order = [((block ^ place) // inner, (block ^ place) % inner) for block in range(blocks)]
        sums[...] = jnp.zeros_like(sums)
        @pl.when(core >= 0)
        def _():
            add_beams(sums, straight[...], order, mine_weight)
            add_beams(sums, far[...], order, other_weight)

        beam_store = pltpu.make_async_copy(sums, beam_ref.at[:, slot], load_sems.at[0])
        beam_store.start()
    if 1 in halves:
        correlate_half(1, far)
    for store in stores[-buffers:]:
        store.wait()
    if with_beams:
        beam_store.wait()


def correlate(where, mine, other, halves, index, weights, slot, slots, beams, earlier):
    blocks, _, _, size, _ = mine.shape
    width = blocks * size
    any_spec = pl.BlockSpec(memory_space=pl.ANY)
    in_specs = [pl.BlockSpec((blocks, None, 2, size, MD), lambda i, where: (0, index, 0, 0, 0))]
    operands = [where, mine]
    if 1 in halves:
        in_specs.append(any_spec)
        operands.append(other)
    scratch = [
        pltpu.VMEM((width, 2 * MD), jnp.bfloat16),
        pltpu.VMEM((width, 2 * MD), jnp.bfloat16),
        pltpu.VMEM((blocks, 2, size, MD), jnp.bfloat16),
        pltpu.VMEM((width, 2 * MD), jnp.bfloat16),
        pltpu.VMEM((STAGES, width, width), jnp.bfloat16),
        pltpu.SemaphoreType.DMA((3,)),
        pltpu.SemaphoreType.DMA((STAGES,)),
    ]
    if weights is not None:
        in_specs += [any_spec] * 2
        operands += list(weights)
        scratch.append(pltpu.VMEM((2, beams, MD), jnp.float32))
        scratch += [pltpu.VMEM(weights[1].shape, jnp.bfloat16)] * 2
    aliases = {}
    if earlier is not None:
        aliases = {len(operands): 0, len(operands) + 1: 1}
        in_specs += [any_spec] * 2
        operands += list(earlier)
    return pl.pallas_call(
        functools.partial(correlate_body, halves, index, slot, weights is not None),
        grid_spec=pltpu.PrefetchScalarGridSpec(
            num_scalar_prefetch=1,
            grid=(1,),
            in_specs=in_specs,
            out_specs=[any_spec, any_spec],
            scratch_shapes=scratch,
        ),
        out_shape=[
            jax.ShapeDtypeStruct((slots, 2, 2 * width, width), jnp.bfloat16),
            jax.ShapeDtypeStruct((2, slots, beams, MD), jnp.float32),
        ],
        input_output_aliases=aliases,
        compiler_params=pltpu.CompilerParams(vmem_limit_bytes=VMEM_LIMIT),
        cost_estimate=pl.CostEstimate(
            flops=8 * len(halves) * MD * width * width, bytes_accessed=5 * len(halves) * width * width, transcendentals=0
        ),
        name="correlate",
    )(*operands)


def exchange(values, axis, turn):
    count = lax.axis_size(axis)
    return lax.ppermute(values, axis, [(index, index ^ turn) for index in range(count)])


def spread_start(weight, ready, inner):
    stations = lax.axis_size("stn")
    outer = stations // inner
    if outer != 4:
        place = lax.axis_index("stn")
        gathered = jnp.take(lax.all_gather(weight, "stn"), place ^ jnp.arange(stations), axis=0)
        return gathered.reshape((outer, inner) + weight.shape), ready
    opposite, ready = lax.optimization_barrier((exchange(weight, "stn", 2 * inner), ready))
    pair = jnp.stack([weight, opposite])
    return (pair, exchange(pair, "stn", 1), exchange(pair, "stn", inner)), ready


def spread_middle(held, inner):
    if not isinstance(held, tuple):
        return held
    return held + (exchange(held[2], "stn", 1),)


def spread_finish(held):
    if not isinstance(held, tuple):
        return held
    pair, beside, side, across = held
    return jnp.stack(
        [
            jnp.stack([pair[0], beside[0]]),
            jnp.stack([side[0], across[0]]),
            jnp.stack([pair[1], beside[1]]),
            jnp.stack([side[1], across[1]]),
        ]
    )


def per_device(raw_samples, prototype, beam_weight):
    stations = lax.axis_size("stn")
    core = lax.axis_index("tile")
    inner = 2
    slots = FINE * DUMPS // stations
    per_dump = max(1, slots // DUMPS)
    turn = functools.partial(lax.all_to_all, axis_name="stn", split_axis=0, concat_axis=0, tiled=True)

    raw_turned = raw_samples.transpose(0, 2, 1)
    spectra = [channelize(raw_turned, prototype, 0, per_dump, True)]
    spread, raw_turned = spread_start(beam_weight, raw_turned, inner)
    spectra += [channelize(raw_turned, prototype, dump, per_dump, False) for dump in range(1, DUMPS)]
    if slots >= DUMPS:
        chunks = [(part, [DUMPS * index for index in range(per_dump)]) for part in spectra[0]]
        chunks += [(part, [DUMPS * index + 1]) for index, part in enumerate(spectra[1])]
    else:
        whole = jnp.stack([spectra[dump][0] for dump in range(DUMPS)], axis=1)
        chunks = [(whole.reshape((stations,) + whole.shape[2:]), [0])]

    half_beams = beam_weight.shape[1] // 2
    where = jnp.stack([core, lax.axis_index("stn")]).astype(jnp.int32)

    outputs = weights = None
    waiting = []
    before = [chunk for chunk, _ in chunks[1:]]
    arrived = turn(chunks[0][0])
    for number, (_, held) in enumerate(chunks):
        final = number + 1 == len(chunks)
        if weights is None:
            mine, before, spread = lax.optimization_barrier((arrived, before, spread))
            if number == 0:
                spread = spread_middle(spread, inner)
        else:
            mine, before = lax.optimization_barrier((arrived, before))
        if not final:
            arrived = turn(chunks[number + 1][0] if number else before[0])
        other = exchange(mine, "tile", 1)
        if weights is None and (number == 1 or final):
            spread = spread_finish(spread)
            give = lax.dynamic_slice_in_dim(spread, (1 - core) * half_beams, half_beams, 3)
            weights = (spread, exchange(give, "tile", 1))
        for index, slot in enumerate(held):
            fused = weights if final else None
            outputs = correlate(where, mine, other, (0, 1), index, fused, slot, slots, half_beams, outputs)
        if not final:
            waiting.append((mine, other, held))
        if weights is not None:
            if waiting:
                outputs = (outputs[0], form_beams(where, waiting, weights, outputs[1]))
            waiting = []
        outputs = before = lax.optimization_barrier(tuple(outputs))
    return tuple(outputs)


def solution(mesh):
    placed = (P(None, ("band", "stn", "tile"), None), P(), P(None, None, ("band", "stn", "tile")))
    return jax.shard_map(
        per_device,
        mesh=mesh,
        in_specs=placed,
        out_specs=(P(("band", "stn"), None, None, "tile"), P(None, ("band", "stn"), "tile", None)),
        check_vma=False,
    )
```
